128 devices in a mesh: row: 8 (over z, core), col: 16 (over y, x).
Axes of the slice: x: 4, y: 4, z: 4, core: 2. Of those that a mesh axis runs over, the one named last changes fastest.
Arguments:
- panel: bfloat16 [64, 131072], P(None, ('row', 'col')), may hold values from -6 to 6
- block_values: bfloat16 [65536, 4096], P(('row', 'col')), may hold values from 0 to 0.049804688
- row_starts: int32 [32768], P(('row', 'col')), may hold values from 0 to 512, as said below
- block_columns: int32 [65536], P(('row', 'col')), may hold values from 0 to 127, as said below
- block_counts: int32 [128], P(('row', 'col')), may hold values from 128 to 512, as said below
Outputs:
- basis: float32 [64, 131072], P(None, ('row', 'col'))
- factor: float32 [64, 64], replicated
The draws below stay inside these ranges and needn't reach their ends.
Inputs may be any that keep to these rules, and one draw needn't show every extreme that they name: `block_counts`: each device's count of stored blocks; some device fills all 512 slots, and column bands differ in load. `row_starts`: within each device's 256 entries the starts do not fall, the first is 0 and none passes that device's block count. `block_columns`: block columns within a device's band.
All inputs are finite; a program needn't handle non-finite values.
Results may differ from the reference program's by a relative error of at most 0.011.
Values may be sent and summed in bfloat16 or wider, within the bound.
No kernel may reach another device: no remote copies, remote signals or barrier semaphores. Data moves between devices by JAX's collectives and lax.ppermute only.
A program may use at most 64 MiB of HBM per device.

```python
import jax
import jax.numpy as jnp
from jax import lax

K = 64
BS = 64
CAP = 512
N = 131072
RBLK = 256
CBLK = 128
N_ROW = 8
N_COL = 16
DEVICES = 128


def block_layout(key):
    device_ids = jnp.arange(DEVICES)
    row_band = device_ids // N_COL
    col_band = device_ids % N_COL
    ratio = N_COL // N_ROW
    low_band = row_band * ratio
    high_band = low_band + ratio - 1
    distance = jnp.maximum(jnp.maximum(low_band - col_band, col_band - high_band), 0)
    spread = (CAP - CAP // 4) // (1 + distance) + 1
    raw = jax.random.randint(jax.random.fold_in(key, 11), (DEVICES,), 0, CAP + 1)
    counts = CAP // 4 + raw % spread
    busiest = jax.random.randint(jax.random.fold_in(key, 12), (), 0, DEVICES)
    lightest = (busiest + 1) % DEVICES
    counts = jnp.where(device_ids == busiest, CAP, counts)
    counts = jnp.where(device_ids == lightest, CAP // 4, counts).astype(jnp.int32)
    block_rows = jax.random.randint(jax.random.fold_in(key, 13), (DEVICES, CAP), 0, RBLK)
    lower_rows = jax.random.randint(jax.random.fold_in(key, 14), (DEVICES, CAP), 0, RBLK - 1)
    block_rows = jnp.where((device_ids == busiest)[:, None], lower_rows, block_rows)
    live = jnp.arange(CAP)[None, :] < counts[:, None]
    below = (block_rows[:, :, None] < jnp.arange(RBLK)[None, None, :]) & live[:, :, None]
    starts = jnp.sum(below.astype(jnp.int32), axis=1).astype(jnp.int32)
    sorted_rows = jnp.sum((starts[:, None, :] <= jnp.arange(CAP)[None, :, None]).astype(jnp.int32), axis=2) - 1
    return (counts, starts.reshape(DEVICES * RBLK), sorted_rows)


def draw_block_counts(key, part):
    counts, starts, rows = block_layout(key)
    return counts


def draw_row_starts(key, part):
    counts, starts, rows = block_layout(key)
    return starts


def draw_block_columns(key, part):
    counts, starts, rows = block_layout(key)
    key = jax.random.fold_in(key, 21)
    device_ids = jnp.arange(DEVICES)
    row_band = device_ids // N_COL
    col_band = device_ids % N_COL
    diagonal = row_band[:, None] * RBLK + rows - col_band[:, None] * CBLK
    near = jnp.clip(diagonal + jax.random.randint(jax.random.fold_in(key, 1), (DEVICES, CAP), -3, 4), 0, CBLK - 1)
    far = jax.random.randint(jax.random.fold_in(key, 2), (DEVICES, CAP), 0, CBLK)
    pick = jax.random.randint(jax.random.fold_in(key, 3), (DEVICES, CAP), 0, 10) < 7
    return jnp.where(pick, near, far).astype(jnp.int32).reshape(DEVICES * CAP)


def levels(rng, dims, split, smallest, high):
    factor_of, own = 1.0, jax.random.fold_in(rng, 6)
    for position, shards_of in split:
        draws = jnp.exp(jax.random.uniform(jax.random.fold_in(own, position), (shards_of,), jnp.float32, smallest / len(split), high / len(split)))
        factor_of = factor_of * jnp.repeat(draws, dims[position] // shards_of).reshape([-1 if axis == position else 1 for axis in range(len(dims))])
    return factor_of


def scatter_about(key, shape, deviation, reach, pieces=(), kind=jnp.bfloat16):
    drawn = deviation * jax.random.normal(key, shape, jnp.float32)
    if pieces:
        drawn = drawn * levels(key, shape, pieces, -0.22, 0.18)
    return jnp.clip(drawn, -reach, reach).astype(kind)


def setup_inputs(seed: int = 0) -> dict:
    streams_of = jax.random.split(jax.random.key(seed), 6)
    panel = scatter_about(streams_of[0], (K, N), 1.0, 6.0, ((1, 128),))
    block_values = jnp.clip(0.049804688 * jax.random.uniform(streams_of[1], (DEVICES * CAP, BS * BS), jnp.float32) ** levels(streams_of[1], (DEVICES * CAP, BS * BS), ((0, 128),), -0.2, 0.2), 0.0, 0.049804688).astype(jnp.bfloat16)
    row_starts = draw_row_starts(jax.random.fold_in(streams_of[5], 71), 0)
    block_columns = draw_block_columns(jax.random.fold_in(streams_of[5], 71), 0)
    block_counts = draw_block_counts(jax.random.fold_in(streams_of[5], 71), 0)
    return dict(panel=panel, block_values=block_values, row_starts=row_starts, block_columns=block_columns, block_counts=block_counts)


def reference(panel, block_values, row_starts, block_columns, block_counts):
    band = N // N_COL
    tiles_all = panel.reshape(K, N // BS, BS).transpose(1, 0, 2).reshape(N // BS, K * BS)

    def device_term(total, index):
        row_band = index // N_COL
        col_band = index % N_COL
        values = lax.dynamic_slice_in_dim(block_values, index * CAP, CAP, 0).reshape(CAP, BS, BS)
        columns = lax.dynamic_slice_in_dim(block_columns, index * CAP, CAP, 0) + col_band * (band // BS)
        starts = lax.dynamic_slice_in_dim(row_starts, index * RBLK, RBLK, 0)
        count = block_counts[index]
        positions = jnp.arange(CAP, dtype=jnp.int32)
        block_rows = jnp.sum((starts[None, :] <= positions[:, None]).astype(jnp.int32), axis=1) - 1 + row_band * RBLK
        segments = jnp.where(positions < count, block_rows, N // BS).astype(jnp.int32)
        picked = tiles_all[columns].reshape(CAP, K, BS).astype(jnp.float32)
        products = jnp.einsum('gkc,grc->gkr', picked, values.astype(jnp.float32)).reshape(CAP, K * BS)
        term = jax.ops.segment_sum(products, segments, num_segments=N // BS)
        rounded = lax.optimization_barrier(term.astype(jnp.bfloat16))
        return (total + rounded.astype(jnp.float32), None)
    start_total = jnp.zeros((N // BS, K * BS), jnp.float32)
    total, unused = lax.scan(device_term, start_total, jnp.arange(DEVICES, dtype=jnp.int32))
    image = total.reshape(N // BS, K, BS).transpose(1, 0, 2).reshape(K, N) + panel.astype(jnp.float32)
    gram = jnp.dot(image.astype(jnp.float32), image.T.astype(jnp.float32), precision=lax.Precision.HIGHEST, preferred_element_type=jnp.float32) / N
    factor = jnp.linalg.cholesky(gram)
    basis = jax.scipy.linalg.solve_triangular(factor, image, lower=True)
    return (basis, factor)
```

```python
import jax
import jax.numpy as jnp
from jax import lax
from jax.experimental import pallas as pl
from jax.experimental.pallas import tpu as pltpu
from jax.sharding import Mesh
from jax.sharding import PartitionSpec as P

K = 64
BS = 64
CAP = 512
RBLK = 256
CBLK = 128
PIECE = 1024
POINTS = 131072
COLS = 16
HALF = BS // 2
UNROLL = 8
AXES = ("z", "core", "y", "x")
ROW = ("z", "core")
COL = ("y", "x")
F32 = jnp.float32
BF16 = jnp.bfloat16


def values_kernel(values, out, spread):
    for group in range(values.shape[0] // 16):
        for tile in range(HALF):
            part = values[group * 16 : (group + 1) * 16, tile * 128 : (tile + 1) * 128]
            spread[pl.ds(tile, 16, stride=HALF), :] = part.astype(F32)
        out[group * 16 * HALF : (group + 1) * 16 * HALF, :] = spread[...].astype(BF16)


def relayout_values(block_values):
    step = 64
    return pl.pallas_call(
        values_kernel,
        grid=(CAP // step,),
        in_specs=[pl.BlockSpec((step, BS * BS), lambda i: (i, 0))],
        out_specs=pl.BlockSpec((step * HALF, 128), lambda i: (i, 0)),
        out_shape=jax.ShapeDtypeStruct((CAP * HALF, 128), BF16),
        scratch_shapes=[pltpu.VMEM((16 * HALF, 128), F32)],
        compiler_params=pltpu.CompilerParams(vmem_limit_bytes=16 * 1024 * 1024),
        cost_estimate=pl.CostEstimate(flops=0, bytes_accessed=8 * 1024 * 1024, transcendentals=0),
    )(block_values)


def multiply_kernel(rows, tiles, rounds, band, values, out, weights, total):
    low = lax.broadcasted_iota(jnp.int32, (K, 128), 1) < BS
    zero = jnp.zeros((K, 128), F32)

    def fill(piece, carry):
        for lane in range(PIECE // 128):
            pair = band[piece, :, lane * 128 : (lane + 1) * 128].astype(F32)
            swapped = pltpu.roll(pair, BS, 1)
            first = pl.multiple_of((piece * (PIECE // BS) + 2 * lane) * 128, 128)
            weights[pl.ds(first, 64), :] = jnp.where(low, pair, zero).astype(BF16)
            weights[pl.ds(first + 64, 64), :] = jnp.where(low, zero, swapped).astype(BF16)
            weights[pl.ds(first + 128, 64), :] = jnp.where(low, swapped, zero).astype(BF16)
            weights[pl.ds(first + 192, 64), :] = jnp.where(low, zero, pair).astype(BF16)
        return carry

    lax.fori_loop(0, band.shape[0], fill, 0)
    total[...] = jnp.zeros_like(total)

    def add_group(index, carry):
        products = []
        for offset in range(UNROLL):
            slot = index * UNROLL + offset
            block = values[pl.ds(pl.multiple_of(slot * HALF, HALF), HALF), :]
            tile = weights[pl.ds(pl.multiple_of(tiles[slot] * 128, 128), 128), :]
            products.append(
                lax.dot_general(block, tile, (((1,), (1,)), ((), ())), preferred_element_type=F32)
            )
        for offset in range(UNROLL):
            slot = index * UNROLL + offset
            place = pl.ds(pl.multiple_of(rows[slot] * HALF, HALF), HALF)
            total[place, :] = total[place, :] + products[offset]
        return carry

    lax.fori_loop(0, rounds[0], add_group, 0)
    out[...] = total[: RBLK * HALF, :].astype(BF16)


def multiply(rows, tiles, rounds, band, values):
    smem = pl.BlockSpec(memory_space=pltpu.SMEM)
    vmem = pl.BlockSpec(memory_space=pltpu.VMEM)
    return pl.pallas_call(
        multiply_kernel,
        in_specs=[smem, smem, smem, vmem, vmem],
        out_specs=vmem,
        out_shape=jax.ShapeDtypeStruct((RBLK * HALF, 128), BF16),
        scratch_shapes=[
            pltpu.VMEM((CBLK * 128, 128), BF16),
            pltpu.VMEM(((RBLK + 1) * HALF, 128), F32),
        ],
        compiler_params=pltpu.CompilerParams(vmem_limit_bytes=40 * 1024 * 1024),
        cost_estimate=pl.CostEstimate(
            flops=2 * CAP * BS * BS * K, bytes_accessed=8 * 1024 * 1024, transcendentals=0
        ),
    )(rows, tiles, rounds, band, values)


def image_kernel(parts, panel, image, gram, spread):
    total = parts[0].astype(F32)
    for index in range(1, COLS):
        total = total + parts[index].astype(F32)
    points = total.shape[0]
    spread[pl.ds(0, points, stride=2), :] = total
    spread[pl.ds(1, points, stride=2), :] = pltpu.roll(total, BS, 1)
    whole = spread[...].T[:K, :] + panel[...].astype(F32)
    image[...] = whole
    gram[...] = lax.dot_general(
        whole,
        whole,
        (((1,), (1,)), ((), ())),
        precision=lax.Precision.HIGHEST,
        preferred_element_type=F32,
    ) * (1.0 / POINTS)


def finish_image(parts, panel):
    vmem = pl.BlockSpec(memory_space=pltpu.VMEM)
    return pl.pallas_call(
        image_kernel,
        in_specs=[vmem, vmem],
        out_specs=[vmem, vmem],
        out_shape=[
            jax.ShapeDtypeStruct((K, PIECE), F32),
            jax.ShapeDtypeStruct((K, K), F32),
        ],
        scratch_shapes=[pltpu.VMEM((PIECE, 128), F32)],
        compiler_params=pltpu.CompilerParams(vmem_limit_bytes=16 * 1024 * 1024),
    )(parts, panel)


def gather_band(panel):
    pieces = []
    for turn in range(4):
        pairs = []
        for z in range(4):
            for core in range(2):
                for col in range(COLS):
                    piece = core * 4 + (z - turn) % 4
                    source = (col // 2) * COLS + 8 * (col % 2) + piece
                    pairs.append((source, (z * 2 + core) * COLS + col))
        pieces.append(lax.ppermute(panel, AXES, pairs))
    own = jnp.stack(pieces)
    return lax.all_gather(own, "core", axis=0, tiled=True)


def sum_along(value, axis, size):
    arrived = [
        lax.ppermute(value, axis, [(i, (i + shift) % size) for i in range(size)])
        for shift in range(1, size)
    ]
    if size == 2:
        return value + arrived[0]
    return (value + arrived[1]) + (arrived[0] + arrived[2])


def per_device(panel, block_values, row_starts, block_columns, block_counts):
    band = gather_band(panel)
    values = relayout_values(block_values)
    positions = lax.iota(jnp.int32, CAP)
    block_rows = jnp.sum((row_starts[None, :] <= positions[:, None]).astype(jnp.int32), axis=1) - 1
    count = block_counts[0]
    rows = jnp.where(positions < count, block_rows, RBLK)
    piece = block_columns // (PIECE // BS)
    turn = (lax.axis_index("z") - piece) % 4
    tiles = ((piece // 4) * 4 + turn) * (PIECE // BS) + block_columns % (PIECE // BS)
    rounds = (block_counts + UNROLL - 1) // UNROLL
    partial = multiply(rows, tiles, rounds, band, values)
    parts = lax.all_to_all(
        partial.reshape(COLS, PIECE // 2, 128), COL, split_axis=0, concat_axis=0, tiled=True
    )
    image, gram = finish_image(parts, panel)
    gram = sum_along(gram, "core", 2)
    for axis in ("x", "y", "z"):
        gram = sum_along(gram, axis, 4)
    factor = jnp.linalg.cholesky(gram)
    basis = jax.scipy.linalg.solve_triangular(factor, image, lower=True)
    return (basis, factor)


def solution(mesh):
    fine = Mesh(mesh.devices.reshape(4, 2, 4, 4), AXES)
    in_specs = (P(None, AXES), P(AXES, None), P(AXES), P(AXES), P(AXES))
    out_specs = (P(None, AXES), P())
    return jax.shard_map(
        per_device, mesh=fine, in_specs=in_specs, out_specs=out_specs, check_vma=False
    )
```

```python
import jax
import jax.numpy as jnp
from jax import lax
from jax.experimental import pallas as pl
from jax.experimental.pallas import tpu as pltpu
from jax.sharding import Mesh
from jax.sharding import PartitionSpec as P

K = 64
BS = 64
CAP = 512
RBLK = 256
CBLK = 128
PIECE = 1024
POINTS = 131072
COLS = 16
HALF = BS // 2
PART = 256
UNROLL = 8
AXES = ("z", "core", "y", "x")
F32 = jnp.float32
BF16 = jnp.bfloat16


def values_kernel(values, out, token, spread):
    for group in range(values.shape[0] // 16):
        for tile in range(HALF):
            part = values[group * 16 : (group + 1) * 16, tile * 128 : (tile + 1) * 128]
            spread[pl.ds(tile, 16, stride=HALF), :] = part.astype(F32)
        out[group * 16 * HALF : (group + 1) * 16 * HALF, :] = spread[...].astype(BF16)
    token[...] = jnp.zeros_like(token)


def relayout_values(block_values):
    step = 64
    return pl.pallas_call(
        values_kernel,
        grid=(CAP // step,),
        in_specs=[pl.BlockSpec((step, BS * BS), lambda i: (i, 0))],
        out_specs=[
            pl.BlockSpec((step * HALF, 128), lambda i: (i, 0)),
            pl.BlockSpec((K, 128), lambda i: (0, 0)),
        ],
        out_shape=[
            jax.ShapeDtypeStruct((CAP * HALF, 128), BF16),
            jax.ShapeDtypeStruct((K, 128), BF16),
        ],
        scratch_shapes=[pltpu.VMEM((16 * HALF, 128), F32)],
        compiler_params=pltpu.CompilerParams(vmem_limit_bytes=16 * 1024 * 1024),
        cost_estimate=pl.CostEstimate(flops=0, bytes_accessed=24 * 1024 * 1024, transcendentals=0),
    )(block_values)


def multiply_kernel(place, rows, tiles, rounds, own, other, stored, *rest):
    outs, (weights, total, values, sem) = rest[:8], rest[8:]
    copy = pltpu.make_async_copy(stored, values, sem)
    copy.start()
    low = lax.broadcasted_iota(jnp.int32, (K, 128), 1) < BS
    zero = jnp.zeros((K, 128), F32)

    for side, band in enumerate((own, other)):

        def fill(piece, carry):
            for lane in range(PIECE // 128):
                pair = band[piece, :, lane * 128 : (lane + 1) * 128].astype(F32)
                swapped = pltpu.roll(pair, BS, 1)
                tile = (side * 4 + piece) * (PIECE // BS) + 2 * lane
                first = pl.multiple_of(tile * 128, 128)
                weights[pl.ds(first, 64), :] = jnp.where(low, pair, zero).astype(BF16)
                weights[pl.ds(first + 64, 64), :] = jnp.where(low, zero, swapped).astype(BF16)
                weights[pl.ds(first + 128, 64), :] = jnp.where(low, swapped, zero).astype(BF16)
                weights[pl.ds(first + 192, 64), :] = jnp.where(low, zero, pair).astype(BF16)
            return carry

        lax.fori_loop(0, 4, fill, 0)
    total[...] = jnp.zeros_like(total)
    copy.wait()

    def add_group(index, carry):
        products = []
        for offset in range(UNROLL):
            slot = index * UNROLL + offset
            block = values[pl.ds(pl.multiple_of(slot * HALF, HALF), HALF), :]
            tile = weights[pl.ds(pl.multiple_of(tiles[slot] * 128, 128), 128), :]
            products.append(
                lax.dot_general(block, tile, (((1,), (1,)), ((), ())), preferred_element_type=F32)
            )
        for offset in range(UNROLL):
            slot = index * UNROLL + offset
            where = pl.ds(pl.multiple_of(rows[slot] * HALF, HALF), HALF)
            total[where, :] = total[where, :] + products[offset]
        return carry

    lax.fori_loop(0, rounds[0], add_group, 0)
    y, x = place[0], place[1]
    for shift in range(4):
        to_x = lax.rem(x + shift, 4)
        to_y = lax.rem(y + shift, 4)
        for index in range(4):
            first = pl.multiple_of((index * 4 + to_x) * 2 * PART, PART)
            outs[shift][index] = total[pl.ds(first, PART), :].astype(BF16)
            first = pl.multiple_of((to_y * 4 + index) * 2 * PART + PART, PART)
            outs[4 + shift][index] = total[pl.ds(first, PART), :].astype(BF16)


def multiply(place, rows, tiles, rounds, own, other, values):
    smem = pl.BlockSpec(memory_space=pltpu.SMEM)
    vmem = pl.BlockSpec(memory_space=pltpu.VMEM)
    return pl.pallas_call(
        multiply_kernel,
        in_specs=[smem] * 4 + [vmem, vmem, pl.BlockSpec(memory_space=pl.ANY)],
        out_specs=[vmem] * 8,
        out_shape=[jax.ShapeDtypeStruct((4, PART, 128), BF16)] * 8,
        scratch_shapes=[
            pltpu.VMEM((CBLK * 128, 128), BF16),
            pltpu.VMEM(((RBLK + 1) * HALF, 128), F32),
            pltpu.VMEM((CAP * HALF, 128), BF16),
            pltpu.SemaphoreType.DMA,
        ],
        compiler_params=pltpu.CompilerParams(vmem_limit_bytes=40 * 1024 * 1024),
        cost_estimate=pl.CostEstimate(
            flops=2 * CAP * BS * BS * K, bytes_accessed=8 * 1024 * 1024, transcendentals=0
        ),
    )(place, rows, tiles, rounds, own, other, values)


def stage_kernel(place, *refs):
    ins, outs = refs[:8], refs[8:]
    for half in range(2):
        base = place[half]
        for shift in range(4):
            to = lax.rem(base + shift, 4)
            total = ins[half * 4][to].astype(F32)
            for index in range(1, 4):
                total = total + ins[half * 4 + index][to].astype(F32)
            outs[half * 4 + shift][...] = total.astype(outs[half * 4 + shift].dtype)


def stage_sums(place, arrays):
    vmem = pl.BlockSpec(memory_space=pltpu.VMEM)
    shapes = [jax.ShapeDtypeStruct((PART, 128), F32)]
    shapes += [jax.ShapeDtypeStruct((PART, 128), BF16)] * 3
    return pl.pallas_call(
        stage_kernel,
        in_specs=[pl.BlockSpec(memory_space=pltpu.SMEM)] + [vmem] * 8,
        out_specs=[vmem] * 8,
        out_shape=shapes * 2,
        compiler_params=pltpu.CompilerParams(vmem_limit_bytes=16 * 1024 * 1024),
    )(place, *arrays)


def image_kernel(*refs):
    ins, (panel, image, gram, spread) = refs[:8], refs[8:]
    for half in range(2):
        total = ins[half * 4][...]
        for index in range(1, 4):
            total = total + ins[half * 4 + index][...].astype(F32)
        spread[pl.ds(half * 2 * PART, PART, stride=2), :] = total
        spread[pl.ds(half * 2 * PART + 1, PART, stride=2), :] = pltpu.roll(total, BS, 1)
    whole = spread[...].T[:K, :] + panel[...].astype(F32)
    image[...] = whole
    gram[...] = lax.dot_general(
        whole,
        whole,
        (((1,), (1,)), ((), ())),
        precision=lax.Precision.HIGHEST,
        preferred_element_type=F32,
    ) * (1.0 / POINTS)


def finish_image(arrays, panel):
    vmem = pl.BlockSpec(memory_space=pltpu.VMEM)
    return pl.pallas_call(
        image_kernel,
        in_specs=[vmem] * 9,
        out_specs=[vmem, vmem],
        out_shape=[
            jax.ShapeDtypeStruct((K, PIECE), F32),
            jax.ShapeDtypeStruct((K, K), F32),
        ],
        scratch_shapes=[pltpu.VMEM((PIECE, 128), F32)],
        compiler_params=pltpu.CompilerParams(vmem_limit_bytes=16 * 1024 * 1024),
    )(*arrays, panel)


def basis_kernel(g0, g1, g2, g3, image, basis, factor, work):
    gram = (g0[...] + g2[...]) + (g1[...] + g3[...])
    work[...] = jnp.zeros_like(work)
    work[:, :K] = gram
    lane = lax.broadcasted_iota(jnp.int32, (8, 128), 1)
    sub = lax.broadcasted_iota(jnp.int32, (8, 128), 0)
    groups = []
    for g in range(8):
        shifted = pltpu.roll(work[g * 8 : (g + 1) * 8, :], K, 1)
        groups.append(jnp.where(lane == sub + g * 8, 1.0, shifted))
    for b in range(8):
        columns = []
        for j in range(8):
            at = K + b * 8 + j
            columns.append(
                [jnp.broadcast_to(groups[g][:, at : at + 1], (8, 128)) for g in range(b, 8)]
            )
        done = []
        for j in range(8):
            scale = lax.rsqrt(columns[j][0][j : j + 1, :])
            scaled = [c * scale for c in columns[j]]
            columns[j] = scaled
            for later in range(j + 1, 8):
                times = scaled[0][later : later + 1, :]
                columns[later] = [c - s * times for c, s in zip(columns[later], scaled)]
            row = groups[b][j : j + 1, :]
            for before in range(j):
                row = row - columns[before][0][j : j + 1, :] * done[before]
            done.append(row * scale)
        for g in range(b + 1, 8):
            value = groups[g]
            for j in range(8):
                value = value - columns[j][g - b] * done[j]
            groups[g] = value
        for j in range(8):
            work[b * 8 + j : b * 8 + j + 1, :] = done[j]
    final = work[...]
    rows = lax.broadcasted_iota(jnp.int32, (K, 128), 0)
    lanes = lax.broadcasted_iota(jnp.int32, (K, 128), 1)
    upper = jnp.where(lanes - K >= rows, final, 0.0)
    factor[...] = upper.T[K:, :]
    inverse = final[:, :K]
    basis[...] = lax.dot_general(
        inverse,
        image[...],
        (((1,), (0,)), ((), ())),
        precision=lax.Precision.HIGHEST,
        preferred_element_type=F32,
    )


def orthogonalize(grams, image):
    vmem = pl.BlockSpec(memory_space=pltpu.VMEM)
    return pl.pallas_call(
        basis_kernel,
        in_specs=[vmem] * 5,
        out_specs=[vmem, vmem],
        out_shape=[
            jax.ShapeDtypeStruct((K, PIECE), F32),
            jax.ShapeDtypeStruct((K, K), F32),
        ],
        scratch_shapes=[pltpu.VMEM((K, 128), F32)],
        compiler_params=pltpu.CompilerParams(vmem_limit_bytes=16 * 1024 * 1024),
    )(*grams, image)


def shifted(value, axis, shift, size=4):
    return lax.ppermute(value, axis, [(i, (i + shift) % size) for i in range(size)])


def gather_band(panel, token):
    pairs = []
    for z in range(4):
        for core in range(2):
            for y in range(4):
                for x in range(4):
                    source = (z * 2 + core) * COLS + y * 4 + x
                    target = ((z + y + x) % 4 * 2 + y % 2) * COLS + z * 4 + 2 * core + y // 2
                    pairs.append((source, target))
    piece = lax.ppermute(panel, AXES, pairs) + jnp.tile(token, (1, PIECE // 128))
    own = jnp.stack([piece] + [shifted(piece, "z", turn) for turn in range(1, 4)])
    return own, shifted(own, "core", 1, 2)


def sum_along(value, axis):
    near, across, far = (shifted(value, axis, shift) for shift in range(1, 4))
    return (value + across) + (near + far)


def per_device(panel, block_values, row_starts, block_columns, block_counts):
    z, core = lax.axis_index("z"), lax.axis_index("core")
    y, x = lax.axis_index("y"), lax.axis_index("x")
    place = jnp.stack([y, x]).astype(jnp.int32)
    values, token = relayout_values(block_values)
    own, other = gather_band(panel, token)
    positions = lax.iota(jnp.int32, CAP)
    block_rows = jnp.sum((row_starts[None, :] <= positions[:, None]).astype(jnp.int32), axis=1) - 1
    rows = jnp.where(positions < block_counts[0], block_rows, RBLK)
    piece = block_columns // (PIECE // BS)
    side, from_x = piece // 4, piece % 4
    turn = (z - y - (2 * (x % 2) + side) - from_x) % 4
    place_of = jnp.where(side == core, 0, 4) + turn
    tiles = place_of * (PIECE // BS) + block_columns % (PIECE // BS)
    rounds = (block_counts + UNROLL - 1) // UNROLL
    partial = multiply(place, rows, tiles, rounds, own, other, values)
    arrived = [partial[0]] + [shifted(partial[shift], "x", shift) for shift in range(1, 4)]
    arrived += [partial[4]] + [shifted(partial[4 + shift], "y", shift) for shift in range(1, 4)]
    sums = stage_sums(place, arrived)
    arrived = [sums[0]] + [shifted(sums[shift], "y", shift) for shift in range(1, 4)]
    arrived += [sums[4]] + [shifted(sums[4 + shift], "x", shift) for shift in range(1, 4)]
    image, gram = finish_image(arrived, panel)
    gram = gram + shifted(gram, "core", 1, 2)
    gram = sum_along(sum_along(gram, "x"), "y")
    grams = [gram] + [shifted(gram, "z", shift) for shift in range(1, 4)]
    basis, factor = orthogonalize(grams, image)
    return (basis, factor)


def solution(mesh):
    fine = Mesh(mesh.devices.reshape(4, 2, 4, 4), AXES)
    in_specs = (P(None, AXES), P(AXES, None), P(AXES), P(AXES), P(AXES))
    out_specs = (P(None, AXES), P())
    return jax.shard_map(
        per_device, mesh=fine, in_specs=in_specs, out_specs=out_specs, check_vma=False
    )
```

```python
import jax
import jax.numpy as jnp
from jax import lax
from jax.experimental import pallas as pl
from jax.experimental.pallas import tpu as pltpu
from jax.sharding import Mesh
from jax.sharding import PartitionSpec as P

K = 64
BS = 64
CAP = 512
RBLK = 256
CBLK = 128
PIECE = 1024
POINTS = 131072
COLS = 16
HALF = BS // 2
PART = 512
PITCH = 40
UNROLL = 32
AXES = ("z", "core", "y", "x")
F32 = jnp.float32
BF16 = jnp.bfloat16


def values_kernel(starts, counts, values, out, rows, spread):
    @pl.when(pl.program_id(0) == 0)
    def _():
        slots = lax.broadcasted_iota(jnp.int32, (8, 128), 0) * 128
        slots = slots + lax.broadcasted_iota(jnp.int32, (8, 128), 1)

        def count_up(step, total):
            for offset in range(8):
                total = total + jnp.where(slots >= starts[step * 8 + offset], 1, 0)
            return total

        total = lax.fori_loop(0, RBLK // 8, count_up, jnp.full((8, 128), -1, jnp.int32))
        rows[...] = jnp.where(slots < counts[0], total, RBLK)

    for group in range(values.shape[0] // 16):
        for tile in range(HALF):
            part = values[group * 16 : (group + 1) * 16, tile * 128 : (tile + 1) * 128]
            spread[pl.ds(tile, 16, stride=PITCH), :] = part.astype(F32)
        for slot in range(16):
            first = (group * 16 + slot) * HALF
            block = spread[slot * PITCH : slot * PITCH + HALF, :]
            out[first : first + HALF, :] = block.astype(BF16)


def relayout_values(starts, counts, block_values):
    step = 64
    smem = pl.BlockSpec(memory_space=pltpu.SMEM)
    return pl.pallas_call(
        values_kernel,
        grid=(CAP // step,),
        in_specs=[smem, smem, pl.BlockSpec((step, BS * BS), lambda i: (i, 0))],
        out_specs=[
            pl.BlockSpec((step * HALF, 128), lambda i: (i, 0)),
            pl.BlockSpec((8, 128), lambda i: (0, 0)),
        ],
        out_shape=[
            jax.ShapeDtypeStruct((CAP * HALF, 128), BF16),
            jax.ShapeDtypeStruct((8, 128), jnp.int32),
        ],
        scratch_shapes=[pltpu.VMEM((16 * PITCH, 128), F32)],
        compiler_params=pltpu.CompilerParams(vmem_limit_bytes=16 * 1024 * 1024),
        cost_estimate=pl.CostEstimate(flops=0, bytes_accessed=24 * 1024 * 1024, transcendentals=0),
    )(starts, counts, block_values)


def transpose_kernel(panel, rows, out, work):
    work[:K, :] = panel[...].astype(F32)
    work[K:, :] = jnp.zeros_like(work[K:, :])
    points = work[...].T
    low = lax.broadcasted_iota(jnp.int32, (HALF, 128), 1) < BS
    for block in range(PIECE // BS):
        first = points[block * BS : block * BS + HALF, :]
        second = points[block * BS + HALF : (block + 1) * BS, :]
        pair = jnp.where(low, first, pltpu.roll(second, BS, 1))
        out[block * HALF : (block + 1) * HALF, :] = pair.astype(BF16)


def transpose_panel(panel, rows):
    vmem = pl.BlockSpec(memory_space=pltpu.VMEM)
    unread = pl.BlockSpec(memory_space=pl.ANY)
    return pl.pallas_call(
        transpose_kernel,
        in_specs=[vmem, unread],
        out_specs=vmem,
        out_shape=jax.ShapeDtypeStruct((PIECE // 2, 128), BF16),
        scratch_shapes=[pltpu.VMEM((128, PIECE), F32)],
        compiler_params=pltpu.CompilerParams(vmem_limit_bytes=16 * 1024 * 1024),
    )(panel, rows)


def multiply_kernel(rows, tiles, counts, own, other, values, *rest):
    outs, (weights, total) = rest[:4], rest[4:]
    z, core = lax.axis_index("z"), lax.axis_index("core")
    y, x = lax.axis_index("y"), lax.axis_index("x")
    low = lax.broadcasted_iota(jnp.int32, (HALF, 128), 1) < BS
    zero = jnp.zeros((HALF, 128), F32)

    for side, band in enumerate((own, other)):

        side = core if side == 0 else 1 - core
        start = z + 12 - y - 2 * lax.rem(x, 2) - side

        def fill(turn, carry, side=side, start=start, band=band):
            piece = side * 4 + lax.rem(start - turn, 4)
            for block in range(PIECE // BS):
                pair = band[turn, block * HALF : (block + 1) * HALF, :].astype(F32)
                swapped = pltpu.roll(pair, BS, 1)
                tile = piece * (PIECE // BS) + block
                first = pl.multiple_of(tile * 128, 128)
                weights[pl.ds(first, HALF), :] = jnp.where(low, pair, zero).astype(BF16)
                weights[pl.ds(first + 32, HALF), :] = jnp.where(low, swapped, zero).astype(BF16)
                weights[pl.ds(first + 64, HALF), :] = jnp.where(low, zero, swapped).astype(BF16)
                weights[pl.ds(first + 96, HALF), :] = jnp.where(low, zero, pair).astype(BF16)
            return carry

        lax.fori_loop(0, 4, fill, 0)
    total[...] = jnp.zeros_like(total)

    def add_group(index, carry):
        products = []
        for offset in range(UNROLL):
            slot = index * UNROLL + offset
            block = values[pl.ds(pl.multiple_of(slot * HALF, HALF), HALF), :]
            tile = weights[pl.ds(pl.multiple_of(tiles[slot] * 128, 128), 128), :]
            products.append(jnp.dot(block, tile, preferred_element_type=F32))
        for offset in range(UNROLL):
            slot = index * UNROLL + offset
            where = pl.ds(pl.multiple_of(rows[lax.div(slot, 128), lax.rem(slot, 128)] * HALF, HALF), HALF)
            total[where, :] = total[where, :] + products[offset]
        return carry

    rounds = lax.div(counts[0] + UNROLL - 1, UNROLL)
    lax.fori_loop(0, rounds, add_group, 0)
    for shift in range(4):
        to_x = lax.rem(x + shift, 4)
        to_y = lax.rem(y + shift, 4)
        for index in range(4):
            chunk = jnp.where(core == 0, index * 4 + to_x, to_y * 4 + index)
            first = pl.multiple_of(chunk * PART, PART)
            outs[shift][index] = total[pl.ds(first, PART), :].astype(BF16)


def multiply(rows, tiles, counts, own, other, values):
    smem = pl.BlockSpec(memory_space=pltpu.SMEM)
    vmem = pl.BlockSpec(memory_space=pltpu.VMEM)
    return pl.pallas_call(
        multiply_kernel,
        in_specs=[smem] * 3 + [vmem] * 3,
        out_specs=[vmem] * 4,
        out_shape=[jax.ShapeDtypeStruct((4, PART, 128), BF16)] * 4,
        scratch_shapes=[
            pltpu.VMEM((CBLK * 128, 128), BF16),
            pltpu.VMEM(((RBLK + 1) * HALF, 128), F32),
        ],
        compiler_params=pltpu.CompilerParams(vmem_limit_bytes=24 * 1024 * 1024),
        cost_estimate=pl.CostEstimate(
            flops=2 * CAP * BS * BS * K, bytes_accessed=8 * 1024 * 1024, transcendentals=0
        ),
    )(rows, tiles, counts, own, other, values)


def stage_kernel(*refs):
    ins, outs = refs[:4], refs[4:]
    base = jnp.where(lax.axis_index("core") == 0, lax.axis_index("y"), lax.axis_index("x"))
    for shift in range(4):
        to = lax.rem(base + shift, 4)
        total = ins[0][to].astype(F32)
        for index in range(1, 4):
            total = total + ins[index][to].astype(F32)
        outs[shift][...] = total.astype(outs[shift].dtype)


def stage_sums(arrays):
    vmem = pl.BlockSpec(memory_space=pltpu.VMEM)
    shapes = [jax.ShapeDtypeStruct((PART, 128), F32)]
    shapes += [jax.ShapeDtypeStruct((PART, 128), BF16)] * 3
    return pl.pallas_call(
        stage_kernel,
        in_specs=[vmem] * 4,
        out_specs=[vmem] * 4,
        out_shape=shapes,
        compiler_params=pltpu.CompilerParams(vmem_limit_bytes=16 * 1024 * 1024),
    )(*arrays)


def image_kernel(*refs):
    ins, (panel, image, gram, spread) = refs[:4], refs[4:]
    total = ins[0][...]
    for index in range(1, 4):
        total = total + ins[index][...].astype(F32)
    spread[pl.ds(0, PART, stride=2), :] = total
    spread[pl.ds(1, PART, stride=2), :] = pltpu.roll(total, BS, 1)
    whole = spread[...].T[:K, :] + panel[...].astype(F32)
    image[...] = whole
    gram[...] = lax.dot_general(
        whole,
        whole,
        (((1,), (1,)), ((), ())),
        precision=lax.Precision.HIGHEST,
        preferred_element_type=F32,
    ) * (1.0 / POINTS)


def finish_image(arrays, panel):
    vmem = pl.BlockSpec(memory_space=pltpu.VMEM)
    return pl.pallas_call(
        image_kernel,
        in_specs=[vmem] * 5,
        out_specs=[vmem, vmem],
        out_shape=[
            jax.ShapeDtypeStruct((K, PIECE), F32),
            jax.ShapeDtypeStruct((K, K), F32),
        ],
        scratch_shapes=[pltpu.VMEM((PIECE, 128), F32)],
        compiler_params=pltpu.CompilerParams(vmem_limit_bytes=16 * 1024 * 1024),
    )(*arrays, panel)


def basis_kernel(g0, g1, g2, g3, image, basis, factor, work):
    gram = (g0[...] + g2[...]) + (g1[...] + g3[...])
    work[...] = jnp.zeros_like(work)
    work[:, :K] = gram
    lane = lax.broadcasted_iota(jnp.int32, (8, 128), 1)
    sub = lax.broadcasted_iota(jnp.int32, (8, 128), 0)
    groups = []
    for g in range(8):
        shifted = pltpu.roll(work[g * 8 : (g + 1) * 8, :], K, 1)
        groups.append(jnp.where(lane == sub + g * 8, 1.0, shifted))
    for b in range(8):
        columns = []
        for j in range(8):
            at = K + b * 8 + j
            columns.append(
                [jnp.broadcast_to(groups[g][:, at : at + 1], (8, 128)) for g in range(b, 8)]
            )
        done = []
        for j in range(8):
            scale = lax.rsqrt(columns[j][0][j : j + 1, :])
            scaled = [c * scale for c in columns[j]]
            columns[j] = scaled
            for later in range(j + 1, 8):
                times = scaled[0][later : later + 1, :]
                columns[later] = [c - s * times for c, s in zip(columns[later], scaled)]
            row = groups[b][j : j + 1, :]
            for before in range(j):
                row = row - columns[before][0][j : j + 1, :] * done[before]
            done.append(row * scale)
        for g in range(b + 1, 8):
            value = groups[g]
            for j in range(8):
                value = value - columns[j][g - b] * done[j]
            groups[g] = value
        for j in range(8):
            work[b * 8 + j : b * 8 + j + 1, :] = done[j]
    final = work[...]
    rows = lax.broadcasted_iota(jnp.int32, (K, 128), 0)
    lanes = lax.broadcasted_iota(jnp.int32, (K, 128), 1)
    upper = jnp.where(lanes - K >= rows, final, 0.0)
    factor[...] = upper.T[K:, :]
    inverse = final[:, :K]
    basis[...] = lax.dot_general(
        inverse,
        image[...],
        (((1,), (0,)), ((), ())),
        precision=lax.Precision.HIGHEST,
        preferred_element_type=F32,
    )


def orthogonalize(grams, image):
    vmem = pl.BlockSpec(memory_space=pltpu.VMEM)
    return pl.pallas_call(
        basis_kernel,
        in_specs=[vmem] * 5,
        out_specs=[vmem, vmem],
        out_shape=[
            jax.ShapeDtypeStruct((K, PIECE), F32),
            jax.ShapeDtypeStruct((K, K), F32),
        ],
        scratch_shapes=[pltpu.VMEM((K, 128), F32)],
        compiler_params=pltpu.CompilerParams(vmem_limit_bytes=16 * 1024 * 1024),
    )(*grams, image)


def shifted(value, axis, shift, size=4):
    return lax.ppermute(value, axis, [(i, (i + shift) % size) for i in range(size)])


def gather_band(panel, rows):
    pairs = []
    for z in range(4):
        for core in range(2):
            for y in range(4):
                for x in range(4):
                    source = (z * 2 + core) * COLS + y * 4 + x
                    target = ((z + y + x) % 4 * 2 + y % 2) * COLS + z * 4 + 2 * core + y // 2
                    pairs.append((source, target))
    piece = transpose_panel(lax.ppermute(panel, AXES, pairs), rows)
    own = jnp.stack([piece] + [shifted(piece, "z", turn) for turn in range(1, 4)])
    return own, shifted(own, "core", 1, 2)


def across(value, shift, first):
    pairs = []
    for z in range(4):
        for core in range(2):
            for y in range(4):
                for x in range(4):
                    along_x = (core == 0) == first
                    to = y * 4 + (x + shift) % 4 if along_x else (y + shift) % 4 * 4 + x
                    row = (z * 2 + core) * COLS
                    pairs.append((row + y * 4 + x, row + to))
    return lax.ppermute(value, AXES, pairs)


def sum_along(value, axis):
    near, across, far = (shifted(value, axis, shift) for shift in range(1, 4))
    return (value + across) + (near + far)


def per_device(panel, block_values, row_starts, block_columns, block_counts):
    values, rows = relayout_values(row_starts, block_counts, block_values)
    own, other = gather_band(panel, rows)
    partial = multiply(rows, block_columns, block_counts, own, other, values)
    order = (2, 1, 3)
    sums = stage_sums([partial[0]] + [across(partial[shift], shift, True) for shift in order])
    arrived = [sums[0]] + [across(sums[shift], shift, False) for shift in order]
    image, gram = finish_image(arrived, panel)
    gram = gram + shifted(gram, "core", 1, 2)
    gram = sum_along(sum_along(gram, "x"), "y")
    grams = [gram] + [shifted(gram, "z", shift) for shift in range(1, 4)]
    basis, factor = orthogonalize(grams, image)
    return (basis, factor)


def solution(mesh):
    fine = Mesh(mesh.devices.reshape(4, 2, 4, 4), AXES)
    in_specs = (P(None, AXES), P(AXES, None), P(AXES), P(AXES), P(AXES))
    out_specs = (P(None, AXES), P())
    return jax.shard_map(
        per_device, mesh=fine, in_specs=in_specs, out_specs=out_specs, check_vma=False
    )
```

```python
import jax
import jax.numpy as jnp
from jax import lax
from jax.experimental import pallas as pl
from jax.experimental.pallas import tpu as pltpu
from jax.sharding import Mesh
from jax.sharding import PartitionSpec as P

K = 64
BS = 64
CAP = 512
RBLK = 256
CBLK = 128
PIECE = 1024
POINTS = 131072
COLS = 16
HALF = BS // 2
PART = 512
PITCH = 40
UNROLL = 32
AXES = ("z", "core", "y", "x")
F32 = jnp.float32
BF16 = jnp.bfloat16


def values_kernel(starts, counts, values, out, rows, spread):
    @pl.when(pl.program_id(0) == 0)
    def _():
        slots = lax.broadcasted_iota(jnp.int32, (8, 128), 0) * 128
        slots = slots + lax.broadcasted_iota(jnp.int32, (8, 128), 1)

        def count_up(step, total):
            for offset in range(8):
                total = total + jnp.where(slots >= starts[step * 8 + offset], 1, 0)
            return total

        total = lax.fori_loop(0, RBLK // 8, count_up, jnp.full((8, 128), -1, jnp.int32))
        rows[...] = jnp.where(slots < counts[0], total, RBLK)

    for group in range(values.shape[0] // 16):
        for tile in range(HALF):
            part = values[group * 16 : (group + 1) * 16, tile * 128 : (tile + 1) * 128]
            spread[pl.ds(tile, 16, stride=PITCH), :] = part.astype(F32)
        for slot in range(16):
            first = (group * 16 + slot) * HALF
            block = spread[slot * PITCH : slot * PITCH + HALF, :]
            out[first : first + HALF, :] = block.astype(BF16)


def relayout_values(starts, counts, block_values):
    step = 64
    smem = pl.BlockSpec(memory_space=pltpu.SMEM)
    return pl.pallas_call(
        values_kernel,
        grid=(CAP // step,),
        in_specs=[smem, smem, pl.BlockSpec((step, BS * BS), lambda i: (i, 0))],
        out_specs=[
            pl.BlockSpec((step * HALF, 128), lambda i: (i, 0)),
            pl.BlockSpec((8, 128), lambda i: (0, 0)),
        ],
        out_shape=[
            jax.ShapeDtypeStruct((CAP * HALF, 128), BF16),
            jax.ShapeDtypeStruct((8, 128), jnp.int32),
        ],
        scratch_shapes=[pltpu.VMEM((16 * PITCH, 128), F32)],
        compiler_params=pltpu.CompilerParams(vmem_limit_bytes=16 * 1024 * 1024),
        cost_estimate=pl.CostEstimate(flops=0, bytes_accessed=24 * 1024 * 1024, transcendentals=0),
    )(starts, counts, block_values)


def transpose_kernel(panel, rows, out, work):
    work[:K, :] = panel[...].astype(F32)
    work[K:, :] = jnp.zeros_like(work[K:, :])
    points = work[...].T
    low = lax.broadcasted_iota(jnp.int32, (HALF, 128), 1) < BS
    for block in range(PIECE // BS):
        first = points[block * BS : block * BS + HALF, :]
        second = points[block * BS + HALF : (block + 1) * BS, :]
        pair = jnp.where(low, first, pltpu.roll(second, BS, 1))
        out[block * HALF : (block + 1) * HALF, :] = pair.astype(BF16)


def transpose_panel(panel, rows):
    vmem = pl.BlockSpec(memory_space=pltpu.VMEM)
    unread = pl.BlockSpec(memory_space=pl.ANY)
    return pl.pallas_call(
        transpose_kernel,
        in_specs=[vmem, unread],
        out_specs=vmem,
        out_shape=jax.ShapeDtypeStruct((PIECE // 2, 128), BF16),
        scratch_shapes=[pltpu.VMEM((128, PIECE), F32)],
        compiler_params=pltpu.CompilerParams(vmem_limit_bytes=16 * 1024 * 1024),
    )(panel, rows)


def multiply_kernel(rows, tiles, counts, own, other, values, *rest):
    outs, (weights, total) = rest[:4], rest[4:]
    z, core = lax.axis_index("z"), lax.axis_index("core")
    y, x = lax.axis_index("y"), lax.axis_index("x")
    low = lax.broadcasted_iota(jnp.int32, (HALF, 128), 1) < BS
    zero = jnp.zeros((HALF, 128), F32)

    for side, band in enumerate((own, other)):

        side = core if side == 0 else 1 - core
        start = z + 12 - y - 2 * lax.rem(x, 2) - side

        def fill(turn, carry, side=side, start=start, band=band):
            piece = side * 4 + lax.rem(start - turn, 4)
            for block in range(PIECE // BS):
                pair = band[turn, block * HALF : (block + 1) * HALF, :].astype(F32)
                swapped = pltpu.roll(pair, BS, 1)
                tile = piece * (PIECE // BS) + block
                first = pl.multiple_of(tile * 128, 128)
                weights[pl.ds(first, HALF), :] = jnp.where(low, pair, zero).astype(BF16)
                weights[pl.ds(first + 32, HALF), :] = jnp.where(low, swapped, zero).astype(BF16)
                weights[pl.ds(first + 64, HALF), :] = jnp.where(low, zero, swapped).astype(BF16)
                weights[pl.ds(first + 96, HALF), :] = jnp.where(low, zero, pair).astype(BF16)
            return carry

        lax.fori_loop(0, 4, fill, 0)
    total[...] = jnp.zeros_like(total)

    def add_group(index, carry):
        products = []
        for offset in range(UNROLL):
            slot = index * UNROLL + offset
            block = values[pl.ds(pl.multiple_of(slot * HALF, HALF), HALF), :]
            tile = weights[pl.ds(pl.multiple_of(tiles[slot] * 128, 128), 128), :]
            products.append(jnp.dot(block, tile, preferred_element_type=F32))
        for offset in range(UNROLL):
            slot = index * UNROLL + offset
            where = pl.ds(pl.multiple_of(rows[lax.div(slot, 128), lax.rem(slot, 128)] * HALF, HALF), HALF)
            total[where, :] = total[where, :] + products[offset]
        return carry

    rounds = lax.div(counts[0] + UNROLL - 1, UNROLL)
    lax.fori_loop(0, rounds, add_group, 0)
    for shift in range(4):
        to_x = lax.rem(x + shift, 4)
        to_y = lax.rem(y + shift, 4)
        for index in range(4):
            chunk = jnp.where(core == 0, index * 4 + to_x, to_y * 4 + index)
            first = pl.multiple_of(chunk * PART, PART)
            outs[shift][index] = total[pl.ds(first, PART), :].astype(BF16)


def multiply(rows, tiles, counts, own, other, values):
    smem = pl.BlockSpec(memory_space=pltpu.SMEM)
    vmem = pl.BlockSpec(memory_space=pltpu.VMEM)
    return pl.pallas_call(
        multiply_kernel,
        in_specs=[smem] * 3 + [vmem] * 3,
        out_specs=[vmem] * 4,
        out_shape=[jax.ShapeDtypeStruct((4, PART, 128), BF16)] * 4,
        scratch_shapes=[
            pltpu.VMEM((CBLK * 128, 128), BF16),
            pltpu.VMEM(((RBLK + 1) * HALF, 128), F32),
        ],
        compiler_params=pltpu.CompilerParams(vmem_limit_bytes=24 * 1024 * 1024),
        cost_estimate=pl.CostEstimate(
            flops=2 * CAP * BS * BS * K, bytes_accessed=8 * 1024 * 1024, transcendentals=0
        ),
    )(rows, tiles, counts, own, other, values)


def stage_kernel(*refs):
    ins, outs = refs[:4], refs[4:]
    base = jnp.where(lax.axis_index("core") == 0, lax.axis_index("y"), lax.axis_index("x"))
    for shift in range(4):
        to = lax.rem(base + shift, 4)
        total = ins[0][to].astype(F32)
        for index in range(1, 4):
            total = total + ins[index][to].astype(F32)
        outs[shift][...] = total.astype(outs[shift].dtype)


def stage_sums(arrays):
    vmem = pl.BlockSpec(memory_space=pltpu.VMEM)
    shapes = [jax.ShapeDtypeStruct((PART, 128), F32)]
    shapes += [jax.ShapeDtypeStruct((PART, 128), BF16)] * 3
    return pl.pallas_call(
        stage_kernel,
        in_specs=[vmem] * 4,
        out_specs=[vmem] * 4,
        out_shape=shapes,
        compiler_params=pltpu.CompilerParams(vmem_limit_bytes=16 * 1024 * 1024),
    )(*arrays)


def image_kernel(*refs):
    ins, (panel, image, gram, spread, packed) = refs[:4], refs[4:]
    total = ins[0][...]
    for index in range(1, 4):
        total = total + ins[index][...].astype(F32)
    spread[pl.ds(0, PART, stride=2), :] = total
    spread[pl.ds(1, PART, stride=2), :] = pltpu.roll(total, BS, 1)
    whole = spread[...].T[:K, :] + panel[...].astype(F32)
    image[...] = whole
    product = lax.dot_general(
        whole,
        whole,
        (((1,), (1,)), ((), ())),
        precision=lax.Precision.HIGHEST,
        preferred_element_type=F32,
    ) * (1.0 / POINTS)
    packed[:, :K] = product[: K // 2, :]
    packed[:, K:] = product[K // 2 :, :]
    for index in range(COLS):
        gram[index] = packed[...]


def finish_image(arrays, panel):
    vmem = pl.BlockSpec(memory_space=pltpu.VMEM)
    return pl.pallas_call(
        image_kernel,
        in_specs=[vmem] * 5,
        out_specs=[vmem, vmem],
        out_shape=[
            jax.ShapeDtypeStruct((K, PIECE), F32),
            jax.ShapeDtypeStruct((COLS, K // 2, 128), F32),
        ],
        scratch_shapes=[pltpu.VMEM((PIECE, 128), F32), pltpu.VMEM((K // 2, 128), F32)],
        compiler_params=pltpu.CompilerParams(vmem_limit_bytes=16 * 1024 * 1024),
    )(*arrays, panel)


def basis_kernel(g0, g1, g2, g3, image, basis, factor, work):
    gram = (g0[...] + g2[...]) + (g1[...] + g3[...])
    work[...] = jnp.zeros_like(work)
    work[: K // 2, :K] = gram[:, :K]
    work[K // 2 :, :K] = pltpu.roll(gram, K, 1)[:, :K]
    lane = lax.broadcasted_iota(jnp.int32, (8, 128), 1)
    sub = lax.broadcasted_iota(jnp.int32, (8, 128), 0)
    groups = []
    for g in range(8):
        shifted = pltpu.roll(work[g * 8 : (g + 1) * 8, :], K, 1)
        groups.append(jnp.where(lane == sub + g * 8, 1.0, shifted))
    for b in range(8):
        columns = []
        for j in range(8):
            at = K + b * 8 + j
            columns.append(
                [jnp.broadcast_to(groups[g][:, at : at + 1], (8, 128)) for g in range(b, 8)]
            )
        done = []
        for j in range(8):
            scale = lax.rsqrt(columns[j][0][j : j + 1, :])
            scaled = [c * scale for c in columns[j]]
            columns[j] = scaled
            for later in range(j + 1, 8):
                times = scaled[0][later : later + 1, :]
                columns[later] = [c - s * times for c, s in zip(columns[later], scaled)]
            row = groups[b][j : j + 1, :]
            for before in range(j):
                row = row - columns[before][0][j : j + 1, :] * done[before]
            done.append(row * scale)
        for g in range(b + 1, 8):
            value = groups[g]
            for j in range(8):
                value = value - columns[j][g - b] * done[j]
            groups[g] = value
        for j in range(8):
            work[b * 8 + j : b * 8 + j + 1, :] = done[j]
    final = work[...]
    rows = lax.broadcasted_iota(jnp.int32, (K, 128), 0)
    lanes = lax.broadcasted_iota(jnp.int32, (K, 128), 1)
    upper = jnp.where(lanes - K >= rows, final, 0.0)
    factor[...] = upper.T[K:, :]
    inverse = final[:, :K]
    basis[...] = lax.dot_general(
        inverse,
        image[...],
        (((1,), (0,)), ((), ())),
        precision=lax.Precision.HIGHEST,
        preferred_element_type=F32,
    )


def orthogonalize(grams, image):
    vmem = pl.BlockSpec(memory_space=pltpu.VMEM)
    return pl.pallas_call(
        basis_kernel,
        in_specs=[vmem] * 5,
        out_specs=[vmem, vmem],
        out_shape=[
            jax.ShapeDtypeStruct((K, PIECE), F32),
            jax.ShapeDtypeStruct((K, K), F32),
        ],
        scratch_shapes=[pltpu.VMEM((K, 128), F32)],
        compiler_params=pltpu.CompilerParams(vmem_limit_bytes=16 * 1024 * 1024),
    )(*grams, image)


def shifted(value, axis, shift, size=4):
    return lax.ppermute(value, axis, [(i, (i + shift) % size) for i in range(size)])


def gather_band(panel, rows):
    pairs = []
    for z in range(4):
        for core in range(2):
            for y in range(4):
                for x in range(4):
                    source = (z * 2 + core) * COLS + y * 4 + x
                    target = ((z + y + x) % 4 * 2 + y % 2) * COLS + z * 4 + 2 * core + y // 2
                    pairs.append((source, target))
    piece = transpose_panel(lax.ppermute(panel, AXES, pairs), rows)
    own = jnp.stack([piece] + [shifted(piece, "z", turn) for turn in range(1, 4)])
    return own, shifted(own, "core", 1, 2)


def across(value, shift, first):
    pairs = []
    for z in range(4):
        for core in range(2):
            for y in range(4):
                for x in range(4):
                    along_x = (core == 0) == first
                    to = y * 4 + (x + shift) % 4 if along_x else (y + shift) % 4 * 4 + x
                    row = (z * 2 + core) * COLS
                    pairs.append((row + y * 4 + x, row + to))
    return lax.ppermute(value, AXES, pairs)


def sum_along(value, axis):
    near, across, far = (shifted(value, axis, shift) for shift in range(1, 4))
    return (value + across) + (near + far)


def per_device(panel, block_values, row_starts, block_columns, block_counts):
    values, rows = relayout_values(row_starts, block_counts, block_values)
    own, other = gather_band(panel, rows)
    partial = multiply(rows, block_columns, block_counts, own, other, values)
    order = (2, 1, 3)
    sums = stage_sums([partial[0]] + [across(partial[shift], shift, True) for shift in order])
    arrived = [sums[0]] + [across(sums[shift], shift, False) for shift in order]
    image, gram = finish_image(arrived, panel)
    gram = jnp.sum(lax.all_to_all(gram, ("y", "x"), 0, 0, tiled=True), axis=0)
    gram = gram + shifted(gram, "core", 1, 2)
    grams = [gram] + [shifted(gram, "z", shift) for shift in range(1, 4)]
    basis, factor = orthogonalize(grams, image)
    return (basis, factor)


def solution(mesh):
    fine = Mesh(mesh.devices.reshape(4, 2, 4, 4), AXES)
    in_specs = (P(None, AXES), P(AXES, None), P(AXES), P(AXES), P(AXES))
    out_specs = (P(None, AXES), P())
    return jax.shard_map(
        per_device, mesh=fine, in_specs=in_specs, out_specs=out_specs, check_vma=False
    )
```

```python
import jax
import jax.numpy as jnp
from jax import lax
from jax.experimental import pallas as pl
from jax.experimental.pallas import tpu as pltpu
from jax.sharding import Mesh
from jax.sharding import PartitionSpec as P

K = 64
BS = 64
CAP = 512
RBLK = 256
CBLK = 128
PIECE = 1024
POINTS = 131072
COLS = 16
HALF = BS // 2
PART = 512
PITCH = 40
ORDER = (2, 1, 3, 0)
FIRST = 12
UNROLL = 64
AXES = ("z", "core", "y", "x")
F32 = jnp.float32
BF16 = jnp.bfloat16


def values_kernel(starts, counts, values, out, rows, order, spread):
    @pl.when(pl.program_id(0) == 0)
    def _():
        core, y, x = lax.axis_index("core"), lax.axis_index("y"), lax.axis_index("x")
        sub = lax.broadcasted_iota(jnp.int32, (8, 128), 0)
        lane = lax.broadcasted_iota(jnp.int32, (8, 128), 1)
        slots = sub * 128 + lane
        place = slots
        shift_rows = jnp.zeros_like(slots)
        live = slots < 0
        filled = 0
        steps = []
        for number in range(COLS):
            if number == FIRST:
                steps.append(lax.div(filled + UNROLL - 1, UNROLL))
                filled = steps[0] * UNROLL
            far, index = ORDER[number // 4], number % 4
            to_x, to_y = lax.rem(x + far, 4), lax.rem(y + far, 4)
            chunk = jnp.where(core == 0, index * 4 + to_x, to_y * 4 + index)
            low = starts[chunk * 16]
            after = starts[jnp.minimum(chunk * 16 + 16, RBLK - 1)]
            high = jnp.where(chunk == COLS - 1, counts[0], after)
            here = slots >= filled
            place = jnp.where(here, slots - filled + low, place)
            shift_rows = jnp.where(here, 16 * (number % FIRST) - 16 * chunk, shift_rows)
            live = jnp.logical_or(
                jnp.logical_and(live, jnp.logical_not(here)),
                jnp.logical_and(here, slots < filled + high - low),
            )
            filled = filled + high - low
        steps.append(lax.div(filled - steps[0] * UNROLL + UNROLL - 1, UNROLL))

        def count_up(step, total):
            for offset in range(8):
                total = total + jnp.where(place >= starts[step * 8 + offset], 1, 0)
            return total

        total = lax.fori_loop(0, RBLK // 8, count_up, jnp.full((8, 128), -1, jnp.int32))
        rows[...] = jnp.where(live, total + shift_rows, FIRST * 16)
        place = jnp.where(live, place, 0)
        order[...] = jnp.where(sub == 7, jnp.where(lane == 0, steps[0], steps[1]), place)

    for group in range(values.shape[0] // 16):
        for tile in range(HALF):
            part = values[group * 16 : (group + 1) * 16, tile * 128 : (tile + 1) * 128]
            spread[pl.ds(tile, 16, stride=PITCH), :] = part.astype(F32)
        for slot in range(16):
            first = (group * 16 + slot) * HALF
            block = spread[slot * PITCH : slot * PITCH + HALF, :]
            out[first : first + HALF, :] = block.astype(BF16)


def relayout_values(starts, counts, block_values):
    step = 64
    smem = pl.BlockSpec(memory_space=pltpu.SMEM)
    return pl.pallas_call(
        values_kernel,
        grid=(CAP // step,),
        in_specs=[smem, smem, pl.BlockSpec((step, BS * BS), lambda i: (i, 0))],
        out_specs=[
            pl.BlockSpec((step * HALF, 128), lambda i: (i, 0)),
            pl.BlockSpec((8, 128), lambda i: (0, 0)),
            pl.BlockSpec((8, 128), lambda i: (0, 0)),
        ],
        out_shape=[
            jax.ShapeDtypeStruct((CAP * HALF, 128), BF16),
            jax.ShapeDtypeStruct((8, 128), jnp.int32),
            jax.ShapeDtypeStruct((8, 128), jnp.int32),
        ],
        scratch_shapes=[pltpu.VMEM((16 * PITCH, 128), F32)],
        compiler_params=pltpu.CompilerParams(vmem_limit_bytes=16 * 1024 * 1024),
        cost_estimate=pl.CostEstimate(flops=0, bytes_accessed=24 * 1024 * 1024, transcendentals=0),
    )(starts, counts, block_values)


def transpose_kernel(panel, rows, out, work):
    work[:K, :] = panel[...].astype(F32)
    work[K:, :] = jnp.zeros_like(work[K:, :])
    points = work[...].T
    low = lax.broadcasted_iota(jnp.int32, (HALF, 128), 1) < BS
    for block in range(PIECE // BS):
        first = points[block * BS : block * BS + HALF, :]
        second = points[block * BS + HALF : (block + 1) * BS, :]
        pair = jnp.where(low, first, pltpu.roll(second, BS, 1))
        out[block * HALF : (block + 1) * HALF, :] = pair.astype(BF16)


def transpose_panel(panel, rows):
    vmem = pl.BlockSpec(memory_space=pltpu.VMEM)
    unread = pl.BlockSpec(memory_space=pl.ANY)
    return pl.pallas_call(
        transpose_kernel,
        in_specs=[vmem, unread],
        out_specs=vmem,
        out_shape=jax.ShapeDtypeStruct((PIECE // 2, 128), BF16),
        scratch_shapes=[pltpu.VMEM((128, PIECE), F32)],
        compiler_params=pltpu.CompilerParams(vmem_limit_bytes=16 * 1024 * 1024),
    )(panel, rows)


def fill_weights(own, other, table, weights):
    z, core = lax.axis_index("z"), lax.axis_index("core")
    y, x = lax.axis_index("y"), lax.axis_index("x")
    low = lax.broadcasted_iota(jnp.int32, (HALF, 128), 1) < BS
    zero = jnp.zeros((HALF, 128), F32)

    for side, band in enumerate((own, other)):
        side = core if side == 0 else 1 - core

        def fill(turn, carry, side=side, band=band):
            source = lax.rem(z + 4 - turn, 4) * 2 + side
            piece = table[source * COLS + y * 4 + x]
            for block in range(PIECE // BS):
                pair = band[turn, block * HALF : (block + 1) * HALF, :].astype(F32)
                swapped = pltpu.roll(pair, BS, 1)
                tile = piece * (PIECE // BS) + block
                first = pl.multiple_of(tile * 128, 128)
                weights[pl.ds(first, HALF), :] = jnp.where(low, pair, zero).astype(BF16)
                weights[pl.ds(first + 32, HALF), :] = jnp.where(low, swapped, zero).astype(BF16)
                weights[pl.ds(first + 64, HALF), :] = jnp.where(low, zero, swapped).astype(BF16)
                weights[pl.ds(first + 96, HALF), :] = jnp.where(low, zero, pair).astype(BF16)
            return carry

        lax.fori_loop(0, 4, fill, 0)


def add_products(first, steps, rows, order, tiles, values, weights, total):
    total[...] = jnp.zeros_like(total)

    def add_group(index, carry):
        group = (first + index) * UNROLL
        major, minor = lax.div(group, 128), lax.rem(group, 128)
        products = []
        for offset in range(UNROLL):
            slot = order[major, minor + offset]
            block = values[pl.ds(pl.multiple_of(slot * HALF, HALF), HALF), :]
            tile = weights[pl.ds(pl.multiple_of(tiles[slot] * 128, 128), 128), :]
            products.append(jnp.dot(block, tile, preferred_element_type=F32))
        for offset in range(UNROLL):
            where = pl.ds(pl.multiple_of(rows[major, minor + offset] * HALF, HALF), HALF)
            total[where, :] = total[where, :] + products[offset]
        return carry

    lax.fori_loop(0, steps, add_group, 0)


def write_chunks(total, outs):
    for number, out in enumerate(outs):
        for index in range(4):
            first = (number * 4 + index) * PART
            out[index] = total[first : first + PART, :].astype(BF16)


def first_kernel(rows, order, tiles, table, own, other, values, weights, out0, out1, out2, total):
    fill_weights(own, other, table, weights)
    add_products(0, order[7, 0], rows, order, tiles, values, weights, total)
    write_chunks(total, (out0, out1, out2))


def second_kernel(rows, order, tiles, weights, values, out0, total):
    add_products(order[7, 0], order[7, 1], rows, order, tiles, values, weights, total)
    write_chunks(total, (out0,))


def multiply(rows, tiles, order, own, other, values):
    smem = pl.BlockSpec(memory_space=pltpu.SMEM)
    vmem = pl.BlockSpec(memory_space=pltpu.VMEM)
    chunks = [jax.ShapeDtypeStruct((4, PART, 128), BF16)] * 3
    total = pltpu.VMEM(((FIRST * 16 + 1) * HALF, 128), F32)
    params = pltpu.CompilerParams(vmem_limit_bytes=16 * 1024 * 1024)
    weights, part2, part1, part3 = pl.pallas_call(
        first_kernel,
        in_specs=[smem] * 4 + [vmem] * 3,
        out_specs=[vmem] * 4,
        out_shape=[jax.ShapeDtypeStruct((CBLK * 128, 128), BF16)] + chunks,
        scratch_shapes=[total],
        compiler_params=params,
    )(rows, order, tiles, jnp.array(placement()[1], jnp.int32), own, other, values)
    (part0,) = pl.pallas_call(
        second_kernel,
        in_specs=[smem] * 3 + [vmem] * 2,
        out_specs=[vmem],
        out_shape=chunks[:1],
        scratch_shapes=[total],
        compiler_params=params,
        cost_estimate=pl.CostEstimate(flops=0, bytes_accessed=16 * 1024 * 1024, transcendentals=0),
    )(rows, order, tiles, weights, values)
    return part0, part1, part2, part3


def stage_kernel(*refs):
    ins, outs = refs[:4], refs[4:]
    base = jnp.where(lax.axis_index("core") == 0, lax.axis_index("y"), lax.axis_index("x"))
    for shift in range(4):
        to = lax.rem(base + shift, 4)
        total = ins[0][to].astype(F32)
        for index in range(1, 4):
            total = total + ins[index][to].astype(F32)
        outs[shift][...] = total.astype(outs[shift].dtype)


def stage_sums(arrays):
    vmem = pl.BlockSpec(memory_space=pltpu.VMEM)
    shapes = [jax.ShapeDtypeStruct((PART, 128), F32)]
    shapes += [jax.ShapeDtypeStruct((PART, 128), BF16)] * 3
    return pl.pallas_call(
        stage_kernel,
        in_specs=[vmem] * 4,
        out_specs=[vmem] * 4,
        out_shape=shapes,
        compiler_params=pltpu.CompilerParams(vmem_limit_bytes=16 * 1024 * 1024),
    )(*arrays)


def image_kernel(*refs):
    ins, (panel, image, gram, spread, packed) = refs[:4], refs[4:]
    total = ins[0][...]
    for index in range(1, 4):
        total = total + ins[index][...].astype(F32)
    spread[pl.ds(0, PART, stride=2), :] = total
    spread[pl.ds(1, PART, stride=2), :] = pltpu.roll(total, BS, 1)
    whole = spread[...].T[:K, :] + panel[...].astype(F32)
    image[...] = whole
    product = lax.dot_general(
        whole,
        whole,
        (((1,), (1,)), ((), ())),
        precision=lax.Precision.HIGHEST,
        preferred_element_type=F32,
    ) * (1.0 / POINTS)
    packed[:, :K] = product[: K // 2, :]
    packed[:, K:] = product[K // 2 :, :]
    for index in range(COLS):
        gram[index] = packed[...]


def finish_image(arrays, panel):
    vmem = pl.BlockSpec(memory_space=pltpu.VMEM)
    return pl.pallas_call(
        image_kernel,
        in_specs=[vmem] * 5,
        out_specs=[vmem, vmem],
        out_shape=[
            jax.ShapeDtypeStruct((K, PIECE), F32),
            jax.ShapeDtypeStruct((COLS, K // 2, 128), F32),
        ],
        scratch_shapes=[pltpu.VMEM((PIECE, 128), F32), pltpu.VMEM((K // 2, 128), F32)],
        compiler_params=pltpu.CompilerParams(vmem_limit_bytes=16 * 1024 * 1024),
    )(*arrays, panel)


def basis_kernel(g0, g1, g2, g3, image, basis, factor, work):
    gram = (g0[...] + g2[...]) + (g1[...] + g3[...])
    work[...] = jnp.zeros_like(work)
    work[: K // 2, :K] = gram[:, :K]
    work[K // 2 :, :K] = pltpu.roll(gram, K, 1)[:, :K]
    lane = lax.broadcasted_iota(jnp.int32, (8, 128), 1)
    sub = lax.broadcasted_iota(jnp.int32, (8, 128), 0)
    groups = []
    for g in range(8):
        shifted = pltpu.roll(work[g * 8 : (g + 1) * 8, :], K, 1)
        groups.append(jnp.where(lane == sub + g * 8, 1.0, shifted))
    for b in range(8):
        columns = []
        for j in range(8):
            at = K + b * 8 + j
            columns.append(
                [jnp.broadcast_to(groups[g][:, at : at + 1], (8, 128)) for g in range(b, 8)]
            )
        done = []
        for j in range(8):
            scale = lax.rsqrt(columns[j][0][j : j + 1, :])
            scaled = [c * scale for c in columns[j]]
            columns[j] = scaled
            for later in range(j + 1, 8):
                times = scaled[0][later : later + 1, :]
                columns[later] = [c - s * times for c, s in zip(columns[later], scaled)]
            row = groups[b][j : j + 1, :]
            for before in range(j):
                row = row - columns[before][0][j : j + 1, :] * done[before]
            done.append(row * scale)
        for g in range(b + 1, 8):
            value = groups[g]
            for j in range(8):
                value = value - columns[j][g - b] * done[j]
            groups[g] = value
        for j in range(8):
            work[b * 8 + j : b * 8 + j + 1, :] = done[j]
    final = work[...]
    rows = lax.broadcasted_iota(jnp.int32, (K, 128), 0)
    lanes = lax.broadcasted_iota(jnp.int32, (K, 128), 1)
    upper = jnp.where(lanes - K >= rows, final, 0.0)
    factor[...] = upper.T[K:, :]
    inverse = final[:, :K]
    basis[...] = lax.dot_general(
        inverse,
        image[...],
        (((1,), (0,)), ((), ())),
        precision=lax.Precision.HIGHEST,
        preferred_element_type=F32,
    )


def orthogonalize(grams, image):
    vmem = pl.BlockSpec(memory_space=pltpu.VMEM)
    return pl.pallas_call(
        basis_kernel,
        in_specs=[vmem] * 5,
        out_specs=[vmem, vmem],
        out_shape=[
            jax.ShapeDtypeStruct((K, PIECE), F32),
            jax.ShapeDtypeStruct((K, K), F32),
        ],
        scratch_shapes=[pltpu.VMEM((K, 128), F32)],
        compiler_params=pltpu.CompilerParams(vmem_limit_bytes=16 * 1024 * 1024),
    )(*grams, image)


def shifted(value, axis, shift, size=4):
    return lax.ppermute(value, axis, [(i, (i + shift) % size) for i in range(size)])


def ring(a, b):
    return min((a - b) % 4, (b - a) % 4)


def placement():
    pairs, table = [], [0] * (8 * COLS)
    for y in range(4):
        for x in range(4):
            row = y * 2 + x // 2
            pieces = []
            for piece in range(8):
                from_y, from_x = 2 * (x % 2) + piece // 4, piece % 4
                pieces.append((-ring(from_y, y) - ring(from_x, x), piece, from_y * 4 + from_x))
            places = sorted((ring(z, y), z, core) for z in range(4) for core in range(2))
            for (_, piece, source), (_, z, core) in zip(sorted(pieces), places):
                target = (z * 2 + core) * COLS + y * 4 + x
                pairs.append((row * COLS + source, target))
                table[target] = piece
    return pairs, table


def gather_band(panel, rows):
    piece = transpose_panel(lax.ppermute(panel, AXES, placement()[0]), rows)
    own = jnp.stack([piece] + [shifted(piece, "z", turn) for turn in range(1, 4)])
    return own, shifted(own, "core", 1, 2)


def across(value, shift, first):
    pairs = []
    for z in range(4):
        for core in range(2):
            for y in range(4):
                for x in range(4):
                    along_x = (core == 0) == first
                    to = y * 4 + (x + shift) % 4 if along_x else (y + shift) % 4 * 4 + x
                    row = (z * 2 + core) * COLS
                    pairs.append((row + y * 4 + x, row + to))
    return lax.ppermute(value, AXES, pairs)


def sum_along(value, axis):
    near, across, far = (shifted(value, axis, shift) for shift in range(1, 4))
    return (value + across) + (near + far)


def per_device(panel, block_values, row_starts, block_columns, block_counts):
    values, rows, order = relayout_values(row_starts, block_counts, block_values)
    own, other = gather_band(panel, rows)
    partial = multiply(rows, block_columns, order, own, other, values)
    sums = stage_sums([partial[0]] + [across(partial[shift], shift, True) for shift in ORDER[:3]])
    arrived = [sums[0]] + [across(sums[shift], shift, False) for shift in ORDER[:3]]
    image, gram = finish_image(arrived, panel)
    gram = jnp.sum(lax.all_to_all(gram, ("y", "x"), 0, 0, tiled=True), axis=0)
    gram = gram + shifted(gram, "core", 1, 2)
    grams = [gram] + [shifted(gram, "z", shift) for shift in range(1, 4)]
    basis, factor = orthogonalize(grams, image)
    return (basis, factor)


def solution(mesh):
    fine = Mesh(mesh.devices.reshape(4, 2, 4, 4), AXES)
    in_specs = (P(None, AXES), P(AXES, None), P(AXES), P(AXES), P(AXES))
    out_specs = (P(None, AXES), P())
    return jax.shard_map(
        per_device, mesh=fine, in_specs=in_specs, out_specs=out_specs, check_vma=False
    )
```

```python
import jax
import jax.numpy as jnp
from jax import lax
from jax.experimental import pallas as pl
from jax.experimental.pallas import tpu as pltpu
from jax.sharding import Mesh
from jax.sharding import PartitionSpec as P

K = 64
BS = 64
CAP = 512
RBLK = 256
CBLK = 128
PIECE = 1024
POINTS = 131072
COLS = 16
HALF = BS // 2
PART = 512
PITCH = 40
ORDER = (2, 1, 3, 0)
FIRST = 12
UNROLL = 64
AXES = ("z", "core", "y", "x")
F32 = jnp.float32
BF16 = jnp.bfloat16


def values_kernel(starts, counts, values, out, rows, order, spread):
    @pl.when(pl.program_id(0) == 0)
    def _():
        core, y, x = lax.axis_index("core"), lax.axis_index("y"), lax.axis_index("x")
        sub = lax.broadcasted_iota(jnp.int32, (8, 128), 0)
        lane = lax.broadcasted_iota(jnp.int32, (8, 128), 1)
        slots = sub * 128 + lane
        place = slots
        shift_rows = jnp.zeros_like(slots)
        live = slots < 0
        filled = 0
        steps = []
        for number in range(COLS):
            if number == FIRST:
                steps.append(lax.div(filled + UNROLL - 1, UNROLL))
                filled = steps[0] * UNROLL
            far, index = ORDER[number // 4], number % 4
            to_x, to_y = lax.rem(x + far, 4), lax.rem(y + far, 4)
            chunk = jnp.where(core == 0, index * 4 + to_x, to_y * 4 + index)
            low = starts[chunk * 16]
            after = starts[jnp.minimum(chunk * 16 + 16, RBLK - 1)]
            high = jnp.where(chunk == COLS - 1, counts[0], after)
            here = slots >= filled
            place = jnp.where(here, slots - filled + low, place)
            shift_rows = jnp.where(here, 16 * (number % FIRST) - 16 * chunk, shift_rows)
            live = jnp.logical_or(
                jnp.logical_and(live, jnp.logical_not(here)),
                jnp.logical_and(here, slots < filled + high - low),
            )
            filled = filled + high - low
        steps.append(lax.div(filled - steps[0] * UNROLL + UNROLL - 1, UNROLL))

        def count_up(step, total):
            for offset in range(8):
                total = total + jnp.where(place >= starts[step * 8 + offset], 1, 0)
            return total

        total = lax.fori_loop(0, RBLK // 8, count_up, jnp.full((8, 128), -1, jnp.int32))
        rows[...] = jnp.where(live, total + shift_rows, FIRST * 16)
        place = jnp.where(live, place, 0)
        order[...] = jnp.where(sub == 7, jnp.where(lane == 0, steps[0], steps[1]), place)

    for group in range(values.shape[0] // 16):
        for tile in range(HALF):
            part = values[group * 16 : (group + 1) * 16, tile * 128 : (tile + 1) * 128]
            spread[pl.ds(tile, 16, stride=PITCH), :] = part.astype(F32)
        for slot in range(16):
            first = (group * 16 + slot) * HALF
            block = spread[slot * PITCH : slot * PITCH + HALF, :]
            out[first : first + HALF, :] = block.astype(BF16)


def relayout_values(starts, counts, block_values):
    step = 64
    smem = pl.BlockSpec(memory_space=pltpu.SMEM)
    return pl.pallas_call(
        values_kernel,
        grid=(CAP // step,),
        in_specs=[smem, smem, pl.BlockSpec((step, BS * BS), lambda i: (i, 0))],
        out_specs=[
            pl.BlockSpec((step * HALF, 128), lambda i: (i, 0)),
            pl.BlockSpec((8, 128), lambda i: (0, 0)),
            pl.BlockSpec((8, 128), lambda i: (0, 0)),
        ],
        out_shape=[
            jax.ShapeDtypeStruct((CAP * HALF, 128), BF16),
            jax.ShapeDtypeStruct((8, 128), jnp.int32),
            jax.ShapeDtypeStruct((8, 128), jnp.int32),
        ],
        scratch_shapes=[pltpu.VMEM((16 * PITCH, 128), F32)],
        compiler_params=pltpu.CompilerParams(vmem_limit_bytes=16 * 1024 * 1024),
        cost_estimate=pl.CostEstimate(flops=0, bytes_accessed=24 * 1024 * 1024, transcendentals=0),
    )(starts, counts, block_values)


def transpose_kernel(panel, rows, out, work):
    work[:K, :] = panel[...].astype(F32)
    work[K:, :] = jnp.zeros_like(work[K:, :])
    points = work[...].T
    low = lax.broadcasted_iota(jnp.int32, (HALF, 128), 1) < BS
    for block in range(PIECE // BS):
        first = points[block * BS : block * BS + HALF, :]
        second = points[block * BS + HALF : (block + 1) * BS, :]
        pair = jnp.where(low, first, pltpu.roll(second, BS, 1))
        out[block * HALF : (block + 1) * HALF, :] = pair.astype(BF16)


def transpose_panel(panel, rows):
    vmem = pl.BlockSpec(memory_space=pltpu.VMEM)
    unread = pl.BlockSpec(memory_space=pl.ANY)
    return pl.pallas_call(
        transpose_kernel,
        in_specs=[vmem, unread],
        out_specs=vmem,
        out_shape=jax.ShapeDtypeStruct((PIECE // 2, 128), BF16),
        scratch_shapes=[pltpu.VMEM((128, PIECE), F32)],
        compiler_params=pltpu.CompilerParams(vmem_limit_bytes=16 * 1024 * 1024),
    )(panel, rows)


PIECE_ROWS = PIECE // BS * 128


def piece_place(turn, mine, table):
    z, core = lax.axis_index("z"), lax.axis_index("core")
    y, x = lax.axis_index("y"), lax.axis_index("x")
    side = core if mine else 1 - core
    return table[(lax.rem(z + 4 - turn, 4) * 2 + side) * COLS + y * 4 + x]


def fill_weights(band, place, weights):
    low = lax.broadcasted_iota(jnp.int32, (HALF, 128), 1) < BS
    zero = jnp.zeros((HALF, 128), F32)

    def fill(turn, carry):
        piece = place(turn)
        for block in range(PIECE // BS):
            pair = band[turn, block * HALF : (block + 1) * HALF, :].astype(F32)
            swapped = pltpu.roll(pair, BS, 1)
            tile = piece * (PIECE // BS) + block
            first = pl.multiple_of(tile * 128, 128)
            weights[pl.ds(first, HALF), :] = jnp.where(low, pair, zero).astype(BF16)
            weights[pl.ds(first + 32, HALF), :] = jnp.where(low, swapped, zero).astype(BF16)
            weights[pl.ds(first + 64, HALF), :] = jnp.where(low, zero, swapped).astype(BF16)
            weights[pl.ds(first + 96, HALF), :] = jnp.where(low, zero, pair).astype(BF16)
        return carry

    lax.fori_loop(0, 4, fill, 0)


def own_kernel(own, weights):
    fill_weights(own, lambda turn: turn, weights)


def own_weights(own):
    vmem = pl.BlockSpec(memory_space=pltpu.VMEM)
    return pl.pallas_call(
        own_kernel,
        in_specs=[vmem],
        out_specs=vmem,
        out_shape=jax.ShapeDtypeStruct((4 * PIECE_ROWS, 128), BF16),
        compiler_params=pltpu.CompilerParams(vmem_limit_bytes=16 * 1024 * 1024),
    )(own)


def add_products(first, steps, rows, order, tiles, values, weights, total):
    total[...] = jnp.zeros_like(total)

    def add_group(index, carry):
        group = (first + index) * UNROLL
        major, minor = lax.div(group, 128), lax.rem(group, 128)
        products = []
        for offset in range(UNROLL):
            slot = order[major, minor + offset]
            block = values[pl.ds(pl.multiple_of(slot * HALF, HALF), HALF), :]
            tile = weights[pl.ds(pl.multiple_of(tiles[slot] * 128, 128), 128), :]
            products.append(jnp.dot(block, tile, preferred_element_type=F32))
        for offset in range(UNROLL):
            where = pl.ds(pl.multiple_of(rows[major, minor + offset] * HALF, HALF), HALF)
            total[where, :] = total[where, :] + products[offset]
        return carry

    lax.fori_loop(0, steps, add_group, 0)


def write_chunks(total, outs):
    for number, out in enumerate(outs):
        for index in range(4):
            first = (number * 4 + index) * PART
            out[index] = total[first : first + PART, :].astype(BF16)


def first_kernel(rows, order, tiles, table, other, values, half, weights, out0, out1, out2, total, sems):
    copies = []
    for turn in range(4):
        first = pl.multiple_of(piece_place(turn, True, table) * PIECE_ROWS, PIECE_ROWS)
        source = half.at[pl.ds(turn * PIECE_ROWS, PIECE_ROWS), :]
        target = weights.at[pl.ds(first, PIECE_ROWS), :]
        copies.append(pltpu.make_async_copy(source, target, sems.at[turn]))
    for copy in copies:
        copy.start()
    fill_weights(other, lambda turn: piece_place(turn, False, table), weights)
    for copy in copies:
        copy.wait()
    add_products(0, order[7, 0], rows, order, tiles, values, weights, total)
    write_chunks(total, (out0, out1, out2))


def second_kernel(rows, order, tiles, weights, values, out0, total):
    add_products(order[7, 0], order[7, 1], rows, order, tiles, values, weights, total)
    write_chunks(total, (out0,))


def multiply(rows, tiles, order, own, other, values):
    smem = pl.BlockSpec(memory_space=pltpu.SMEM)
    vmem = pl.BlockSpec(memory_space=pltpu.VMEM)
    chunks = [jax.ShapeDtypeStruct((4, PART, 128), BF16)] * 3
    total = pltpu.VMEM(((FIRST * 16 + 1) * HALF, 128), F32)
    params = pltpu.CompilerParams(vmem_limit_bytes=16 * 1024 * 1024)
    table = jnp.array(placement()[1], jnp.int32)
    half = own_weights(own)
    weights, part2, part1, part3 = pl.pallas_call(
        first_kernel,
        in_specs=[smem] * 4 + [vmem] * 3,
        out_specs=[vmem] * 4,
        out_shape=[jax.ShapeDtypeStruct((CBLK * 128, 128), BF16)] + chunks,
        scratch_shapes=[total, pltpu.SemaphoreType.DMA((4,))],
        compiler_params=params,
    )(rows, order, tiles, table, other, values, half)
    (part0,) = pl.pallas_call(
        second_kernel,
        in_specs=[smem] * 3 + [vmem] * 2,
        out_specs=[vmem],
        out_shape=chunks[:1],
        scratch_shapes=[total],
        compiler_params=params,
        cost_estimate=pl.CostEstimate(flops=0, bytes_accessed=16 * 1024 * 1024, transcendentals=0),
    )(rows, order, tiles, weights, values)
    return part0, part1, part2, part3


def stage_kernel(*refs):
    ins, outs = refs[:4], refs[4:]
    base = jnp.where(lax.axis_index("core") == 0, lax.axis_index("y"), lax.axis_index("x"))
    for shift in range(4):
        to = lax.rem(base + shift, 4)
        total = ins[0][to].astype(F32)
        for index in range(1, 4):
            total = total + ins[index][to].astype(F32)
        outs[shift][...] = total.astype(outs[shift].dtype)


def stage_sums(arrays):
    vmem = pl.BlockSpec(memory_space=pltpu.VMEM)
    shapes = [jax.ShapeDtypeStruct((PART, 128), F32)]
    shapes += [jax.ShapeDtypeStruct((PART, 128), BF16)] * 3
    return pl.pallas_call(
        stage_kernel,
        in_specs=[vmem] * 4,
        out_specs=[vmem] * 4,
        out_shape=shapes,
        compiler_params=pltpu.CompilerParams(vmem_limit_bytes=16 * 1024 * 1024),
    )(*arrays)


def image_kernel(*refs):
    ins, (panel, image, gram, spread, packed) = refs[:4], refs[4:]
    total = ins[0][...]
    for index in range(1, 4):
        total = total + ins[index][...].astype(F32)
    spread[pl.ds(0, PART, stride=2), :] = total
    spread[pl.ds(1, PART, stride=2), :] = pltpu.roll(total, BS, 1)
    whole = spread[...].T[:K, :] + panel[...].astype(F32)
    image[...] = whole
    product = lax.dot_general(
        whole,
        whole,
        (((1,), (1,)), ((), ())),
        precision=lax.Precision.HIGHEST,
        preferred_element_type=F32,
    ) * (1.0 / POINTS)
    packed[:, :K] = product[: K // 2, :]
    packed[:, K:] = product[K // 2 :, :]
    for index in range(COLS):
        gram[index] = packed[...]


def finish_image(arrays, panel):
    vmem = pl.BlockSpec(memory_space=pltpu.VMEM)
    return pl.pallas_call(
        image_kernel,
        in_specs=[vmem] * 5,
        out_specs=[vmem, vmem],
        out_shape=[
            jax.ShapeDtypeStruct((K, PIECE), F32),
            jax.ShapeDtypeStruct((COLS, K // 2, 128), F32),
        ],
        scratch_shapes=[pltpu.VMEM((PIECE, 128), F32), pltpu.VMEM((K // 2, 128), F32)],
        compiler_params=pltpu.CompilerParams(vmem_limit_bytes=16 * 1024 * 1024),
    )(*arrays, panel)


def basis_kernel(g0, g1, g2, g3, image, basis, factor, work):
    gram = (g0[...] + g2[...]) + (g1[...] + g3[...])
    work[...] = jnp.zeros_like(work)
    work[: K // 2, :K] = gram[:, :K]
    work[K // 2 :, :K] = pltpu.roll(gram, K, 1)[:, :K]
    lane = lax.broadcasted_iota(jnp.int32, (8, 128), 1)
    sub = lax.broadcasted_iota(jnp.int32, (8, 128), 0)
    groups = []
    for g in range(8):
        shifted = pltpu.roll(work[g * 8 : (g + 1) * 8, :], K, 1)
        groups.append(jnp.where(lane == sub + g * 8, 1.0, shifted))
    for b in range(8):
        columns = []
        for j in range(8):
            at = K + b * 8 + j
            columns.append(
                [jnp.broadcast_to(groups[g][:, at : at + 1], (8, 128)) for g in range(b, 8)]
            )
        done = []
        for j in range(8):
            scale = lax.rsqrt(columns[j][0][j : j + 1, :])
            scaled = [c * scale for c in columns[j]]
            columns[j] = scaled
            for later in range(j + 1, 8):
                times = scaled[0][later : later + 1, :]
                columns[later] = [c - s * times for c, s in zip(columns[later], scaled)]
            row = groups[b][j : j + 1, :]
            for before in range(j):
                row = row - columns[before][0][j : j + 1, :] * done[before]
            done.append(row * scale)
        for g in range(b + 1, 8):
            value = groups[g]
            for j in range(8):
                value = value - columns[j][g - b] * done[j]
            groups[g] = value
        for j in range(8):
            work[b * 8 + j : b * 8 + j + 1, :] = done[j]
    final = work[...]
    rows = lax.broadcasted_iota(jnp.int32, (K, 128), 0)
    lanes = lax.broadcasted_iota(jnp.int32, (K, 128), 1)
    upper = jnp.where(lanes - K >= rows, final, 0.0)
    factor[...] = upper.T[K:, :]
    inverse = final[:, :K]
    basis[...] = lax.dot_general(
        inverse,
        image[...],
        (((1,), (0,)), ((), ())),
        precision=lax.Precision.HIGHEST,
        preferred_element_type=F32,
    )


def orthogonalize(grams, image):
    vmem = pl.BlockSpec(memory_space=pltpu.VMEM)
    return pl.pallas_call(
        basis_kernel,
        in_specs=[vmem] * 5,
        out_specs=[vmem, vmem],
        out_shape=[
            jax.ShapeDtypeStruct((K, PIECE), F32),
            jax.ShapeDtypeStruct((K, K), F32),
        ],
        scratch_shapes=[pltpu.VMEM((K, 128), F32)],
        compiler_params=pltpu.CompilerParams(vmem_limit_bytes=16 * 1024 * 1024),
    )(*grams, image)


def shifted(value, axis, shift, size=4):
    return lax.ppermute(value, axis, [(i, (i + shift) % size) for i in range(size)])


def ring(a, b):
    return min((a - b) % 4, (b - a) % 4)


def placement():
    pairs, table = [], [0] * (8 * COLS)
    for y in range(4):
        for x in range(4):
            row = y * 2 + x // 2
            pieces = []
            for piece in range(8):
                from_y, from_x = 2 * (x % 2) + piece // 4, piece % 4
                pieces.append((-ring(from_y, y) - ring(from_x, x), piece, from_y * 4 + from_x))
            places = sorted((ring(z, y), z, core) for z in range(4) for core in range(2))
            for (_, piece, source), (_, z, core) in zip(sorted(pieces), places):
                target = (z * 2 + core) * COLS + y * 4 + x
                pairs.append((row * COLS + source, target))
                table[target] = piece
    return pairs, table


def gather_band(panel, rows):
    piece = transpose_panel(lax.ppermute(panel, AXES, placement()[0]), rows)
    own = jnp.stack([piece] + [shifted(piece, "z", turn) for turn in range(1, 4)])
    return own, shifted(own, "core", 1, 2)


def across(value, shift, first):
    pairs = []
    for z in range(4):
        for core in range(2):
            for y in range(4):
                for x in range(4):
                    along_x = (core == 0) == first
                    to = y * 4 + (x + shift) % 4 if along_x else (y + shift) % 4 * 4 + x
                    row = (z * 2 + core) * COLS
                    pairs.append((row + y * 4 + x, row + to))
    return lax.ppermute(value, AXES, pairs)


def sum_along(value, axis):
    near, across, far = (shifted(value, axis, shift) for shift in range(1, 4))
    return (value + across) + (near + far)


def per_device(panel, block_values, row_starts, block_columns, block_counts):
    values, rows, order = relayout_values(row_starts, block_counts, block_values)
    own, other = gather_band(panel, rows)
    partial = multiply(rows, block_columns, order, own, other, values)
    sums = stage_sums([partial[0]] + [across(partial[shift], shift, True) for shift in ORDER[:3]])
    arrived = [sums[0]] + [across(sums[shift], shift, False) for shift in ORDER[:3]]
    image, gram = finish_image(arrived, panel)
    gram = jnp.sum(lax.all_to_all(gram, ("y", "x"), 0, 0, tiled=True), axis=0)
    gram = gram + shifted(gram, "core", 1, 2)
    grams = [gram] + [shifted(gram, "z", shift) for shift in range(1, 4)]
    basis, factor = orthogonalize(grams, image)
    return (basis, factor)


def solution(mesh):
    fine = Mesh(mesh.devices.reshape(4, 2, 4, 4), AXES)
    in_specs = (P(None, AXES), P(AXES, None), P(AXES), P(AXES), P(AXES))
    out_specs = (P(None, AXES), P())
    return jax.shard_map(
        per_device, mesh=fine, in_specs=in_specs, out_specs=out_specs, check_vma=False
    )
```

```python
import jax
import jax.numpy as jnp
from jax import lax
from jax.experimental import pallas as pl
from jax.experimental.pallas import tpu as pltpu
from jax.sharding import Mesh
from jax.sharding import PartitionSpec as P

K = 64
BS = 64
CAP = 512
RBLK = 256
CBLK = 128
PIECE = 1024
POINTS = 131072
COLS = 16
HALF = BS // 2
PART = 512
PITCH = 40
ORDER = (2, 1, 3, 0)
FIRST = 12
UNROLL = 64
AXES = ("z", "core", "y", "x")
F32 = jnp.float32
BF16 = jnp.bfloat16


def values_kernel(starts, counts, values, out, rows, order, spread):
    @pl.when(pl.program_id(0) == 0)
    def _():
        core, y, x = lax.axis_index("core"), lax.axis_index("y"), lax.axis_index("x")
        sub = lax.broadcasted_iota(jnp.int32, (8, 128), 0)
        lane = lax.broadcasted_iota(jnp.int32, (8, 128), 1)
        slots = sub * 128 + lane
        place = slots
        shift_rows = jnp.zeros_like(slots)
        live = slots < 0
        filled = 0
        steps = []
        for number in range(COLS):
            if number == FIRST:
                steps.append(lax.div(filled + UNROLL - 1, UNROLL))
                filled = steps[0] * UNROLL
            far, index = ORDER[number // 4], number % 4
            to_x, to_y = lax.rem(x + far, 4), lax.rem(y + far, 4)
            chunk = jnp.where(core == 0, index * 4 + to_x, to_y * 4 + index)
            low = starts[chunk * 16]
            after = starts[jnp.minimum(chunk * 16 + 16, RBLK - 1)]
            high = jnp.where(chunk == COLS - 1, counts[0], after)
            here = slots >= filled
            place = jnp.where(here, slots - filled + low, place)
            shift_rows = jnp.where(here, 16 * (number % FIRST) - 16 * chunk, shift_rows)
            live = jnp.logical_or(
                jnp.logical_and(live, jnp.logical_not(here)),
                jnp.logical_and(here, slots < filled + high - low),
            )
            filled = filled + high - low
        steps.append(lax.div(filled - steps[0] * UNROLL + UNROLL - 1, UNROLL))

        def count_up(step, total):
            for offset in range(8):
                total = total + jnp.where(place >= starts[step * 8 + offset], 1, 0)
            return total

        total = lax.fori_loop(0, RBLK // 8, count_up, jnp.full((8, 128), -1, jnp.int32))
        rows[...] = jnp.where(live, total + shift_rows, FIRST * 16)
        place = jnp.where(live, place, 0)
        order[...] = jnp.where(sub == 7, jnp.where(lane == 0, steps[0], steps[1]), place)

    for group in range(values.shape[0] // 16):
        for tile in range(HALF):
            part = values[group * 16 : (group + 1) * 16, tile * 128 : (tile + 1) * 128]
            spread[pl.ds(tile, 16, stride=PITCH), :] = part.astype(F32)
        for slot in range(16):
            first = (group * 16 + slot) * HALF
            block = spread[slot * PITCH : slot * PITCH + HALF, :]
            out[first : first + HALF, :] = block.astype(BF16)


def relayout_values(starts, counts, block_values):
    step = 64
    smem = pl.BlockSpec(memory_space=pltpu.SMEM)
    return pl.pallas_call(
        values_kernel,
        grid=(CAP // step,),
        in_specs=[smem, smem, pl.BlockSpec((step, BS * BS), lambda i: (i, 0))],
        out_specs=[
            pl.BlockSpec((step * HALF, 128), lambda i: (i, 0)),
            pl.BlockSpec((8, 128), lambda i: (0, 0)),
            pl.BlockSpec((8, 128), lambda i: (0, 0)),
        ],
        out_shape=[
            jax.ShapeDtypeStruct((CAP * HALF, 128), BF16),
            jax.ShapeDtypeStruct((8, 128), jnp.int32),
            jax.ShapeDtypeStruct((8, 128), jnp.int32),
        ],
        scratch_shapes=[pltpu.VMEM((16 * PITCH, 128), F32)],
        compiler_params=pltpu.CompilerParams(vmem_limit_bytes=16 * 1024 * 1024),
        cost_estimate=pl.CostEstimate(flops=0, bytes_accessed=24 * 1024 * 1024, transcendentals=0),
    )(starts, counts, block_values)


def transpose_kernel(panel, rows, out, work):
    work[:K, :] = panel[...].astype(F32)
    work[K:, :] = jnp.zeros_like(work[K:, :])
    points = work[...].T
    low = lax.broadcasted_iota(jnp.int32, (HALF, 128), 1) < BS
    for block in range(PIECE // BS):
        first = points[block * BS : block * BS + HALF, :]
        second = points[block * BS + HALF : (block + 1) * BS, :]
        pair = jnp.where(low, first, pltpu.roll(second, BS, 1))
        out[block * HALF : (block + 1) * HALF, :] = pair.astype(BF16)


def transpose_panel(panel, rows):
    vmem = pl.BlockSpec(memory_space=pltpu.VMEM)
    unread = pl.BlockSpec(memory_space=pl.ANY)
    return pl.pallas_call(
        transpose_kernel,
        in_specs=[vmem, unread],
        out_specs=vmem,
        out_shape=jax.ShapeDtypeStruct((PIECE // 2, 128), BF16),
        scratch_shapes=[pltpu.VMEM((128, PIECE), F32)],
        compiler_params=pltpu.CompilerParams(vmem_limit_bytes=16 * 1024 * 1024),
    )(panel, rows)


PIECE_ROWS = PIECE // BS * 128


def piece_place(turn, mine, table):
    z, core = lax.axis_index("z"), lax.axis_index("core")
    y, x = lax.axis_index("y"), lax.axis_index("x")
    side = core if mine else 1 - core
    return table[(lax.rem(z + 4 - turn, 4) * 2 + side) * COLS + y * 4 + x]


def fill_weights(band, place, weights):
    low = lax.broadcasted_iota(jnp.int32, (HALF, 128), 1) < BS
    zero = jnp.zeros((HALF, 128), F32)

    def fill(turn, carry):
        piece = place(turn)
        for block in range(PIECE // BS):
            pair = band[turn, block * HALF : (block + 1) * HALF, :].astype(F32)
            swapped = pltpu.roll(pair, BS, 1)
            tile = piece * (PIECE // BS) + block
            first = pl.multiple_of(tile * 128, 128)
            weights[pl.ds(first, HALF), :] = jnp.where(low, pair, zero).astype(BF16)
            weights[pl.ds(first + 32, HALF), :] = jnp.where(low, swapped, zero).astype(BF16)
            weights[pl.ds(first + 64, HALF), :] = jnp.where(low, zero, swapped).astype(BF16)
            weights[pl.ds(first + 96, HALF), :] = jnp.where(low, zero, pair).astype(BF16)
        return carry

    lax.fori_loop(0, 4, fill, 0)


def own_kernel(own, weights):
    fill_weights(own, lambda turn: turn, weights)


def own_weights(own):
    vmem = pl.BlockSpec(memory_space=pltpu.VMEM)
    return pl.pallas_call(
        own_kernel,
        in_specs=[vmem],
        out_specs=vmem,
        out_shape=jax.ShapeDtypeStruct((4 * PIECE_ROWS, 128), BF16),
        compiler_params=pltpu.CompilerParams(vmem_limit_bytes=16 * 1024 * 1024),
    )(own)


def add_products(first, steps, rows, order, tiles, values, weights, total):
    total[...] = jnp.zeros_like(total)

    def add_group(index, carry):
        group = (first + index) * UNROLL
        major, minor = lax.div(group, 128), lax.rem(group, 128)
        products = []
        for offset in range(UNROLL):
            slot = order[major, minor + offset]
            block = values[pl.ds(pl.multiple_of(slot * HALF, HALF), HALF), :]
            tile = weights[pl.ds(pl.multiple_of(tiles[slot] * 128, 128), 128), :]
            products.append(jnp.dot(block, tile, preferred_element_type=F32))
        for offset in range(UNROLL):
            where = pl.ds(pl.multiple_of(rows[major, minor + offset] * HALF, HALF), HALF)
            total[where, :] = total[where, :] + products[offset]
        return carry

    lax.fori_loop(0, steps, add_group, 0)


def write_chunks(total, outs):
    for number, out in enumerate(outs):
        for index in range(4):
            first = (number * 4 + index) * PART
            out[index] = total[first : first + PART, :].astype(BF16)


def first_kernel(rows, order, tiles, table, other, values, half, weights, out0, out1, out2, total, sems):
    copies = []
    for turn in range(4):
        first = pl.multiple_of(piece_place(turn, True, table) * PIECE_ROWS, PIECE_ROWS)
        source = half.at[pl.ds(turn * PIECE_ROWS, PIECE_ROWS), :]
        target = weights.at[pl.ds(first, PIECE_ROWS), :]
        copies.append(pltpu.make_async_copy(source, target, sems.at[turn]))
    for copy in copies:
        copy.start()
    fill_weights(other, lambda turn: piece_place(turn, False, table), weights)
    for copy in copies:
        copy.wait()
    add_products(0, order[7, 0], rows, order, tiles, values, weights, total)
    write_chunks(total, (out0, out1, out2))


def second_kernel(rows, order, tiles, weights, values, out0, total):
    add_products(order[7, 0], order[7, 1], rows, order, tiles, values, weights, total)
    write_chunks(total, (out0,))


def multiply(rows, tiles, order, own, other, values):
    smem = pl.BlockSpec(memory_space=pltpu.SMEM)
    vmem = pl.BlockSpec(memory_space=pltpu.VMEM)
    chunks = [jax.ShapeDtypeStruct((4, PART, 128), BF16)] * 3
    total = pltpu.VMEM(((FIRST * 16 + 1) * HALF, 128), F32)
    params = pltpu.CompilerParams(vmem_limit_bytes=16 * 1024 * 1024)
    table = jnp.array(placement()[1], jnp.int32)
    half = own_weights(own)
    weights, part2, part1, part3 = pl.pallas_call(
        first_kernel,
        in_specs=[smem] * 4 + [vmem] * 3,
        out_specs=[vmem] * 4,
        out_shape=[jax.ShapeDtypeStruct((CBLK * 128, 128), BF16)] + chunks,
        scratch_shapes=[total, pltpu.SemaphoreType.DMA((4,))],
        compiler_params=params,
    )(rows, order, tiles, table, other, values, half)
    (part0,) = pl.pallas_call(
        second_kernel,
        in_specs=[smem] * 3 + [vmem] * 2,
        out_specs=[vmem],
        out_shape=chunks[:1],
        scratch_shapes=[total],
        compiler_params=params,
        cost_estimate=pl.CostEstimate(flops=0, bytes_accessed=16 * 1024 * 1024, transcendentals=0),
    )(rows, order, tiles, weights, values)
    return part0, part1, part2, part3


def stage_kernel(*refs):
    ins, outs = refs[:4], refs[4:]
    base = jnp.where(lax.axis_index("core") == 0, lax.axis_index("y"), lax.axis_index("x"))
    for shift in range(4):
        to = lax.rem(base + shift, 4)
        total = ins[0][to].astype(F32)
        for index in range(1, 4):
            total = total + ins[index][to].astype(F32)
        outs[shift][...] = total.astype(outs[shift].dtype)


def stage_sums(arrays):
    vmem = pl.BlockSpec(memory_space=pltpu.VMEM)
    shapes = [jax.ShapeDtypeStruct((PART, 128), F32)]
    shapes += [jax.ShapeDtypeStruct((PART, 128), BF16)] * 3
    return pl.pallas_call(
        stage_kernel,
        in_specs=[vmem] * 4,
        out_specs=[vmem] * 4,
        out_shape=shapes,
        compiler_params=pltpu.CompilerParams(vmem_limit_bytes=16 * 1024 * 1024),
    )(*arrays)


def image_kernel(*refs):
    ins, (panel, image, gram, spread, packed) = refs[:4], refs[4:]
    total = ins[0][...]
    for index in range(1, 4):
        total = total + ins[index][...].astype(F32)
    spread[pl.ds(0, PART, stride=2), :] = total
    spread[pl.ds(1, PART, stride=2), :] = pltpu.roll(total, BS, 1)
    whole = spread[...].T[:K, :] + panel[...].astype(F32)
    image[...] = whole
    product = lax.dot_general(
        whole,
        whole,
        (((1,), (1,)), ((), ())),
        precision=lax.Precision.HIGHEST,
        preferred_element_type=F32,
    ) * (1.0 / POINTS)
    packed[:, :K] = product[: K // 2, :]
    packed[:, K:] = product[K // 2 :, :]
    for index in range(COLS):
        gram[index] = packed[...]


def finish_image(arrays, panel):
    vmem = pl.BlockSpec(memory_space=pltpu.VMEM)
    return pl.pallas_call(
        image_kernel,
        in_specs=[vmem] * 5,
        out_specs=[vmem, vmem],
        out_shape=[
            jax.ShapeDtypeStruct((K, PIECE), F32),
            jax.ShapeDtypeStruct((COLS, K // 2, 128), F32),
        ],
        scratch_shapes=[pltpu.VMEM((PIECE, 128), F32), pltpu.VMEM((K // 2, 128), F32)],
        compiler_params=pltpu.CompilerParams(vmem_limit_bytes=16 * 1024 * 1024),
    )(*arrays, panel)


def basis_kernel(g0, g1, g2, g3, image, basis, factor, work):
    gram = (g0[...] + g2[...]) + (g1[...] + g3[...])
    work[...] = jnp.zeros_like(work)
    work[: K // 2, :K] = gram[:, :K]
    work[K // 2 :, :K] = pltpu.roll(gram, K, 1)[:, :K]
    lane = lax.broadcasted_iota(jnp.int32, (8, 128), 1)
    sub = lax.broadcasted_iota(jnp.int32, (8, 128), 0)
    groups = []
    for g in range(8):
        shifted = pltpu.roll(work[g * 8 : (g + 1) * 8, :], K, 1)
        groups.append(jnp.where(lane == sub + g * 8, 1.0, shifted))
    for b in range(8):
        columns = []
        for j in range(8):
            at = K + b * 8 + j
            columns.append(
                [jnp.broadcast_to(groups[g][:, at : at + 1], (8, 128)) for g in range(b, 8)]
            )
        done = []
        for j in range(8):
            scale = lax.rsqrt(columns[j][0][j : j + 1, :])
            scaled = [c * scale for c in columns[j]]
            columns[j] = scaled
            for later in range(j + 1, 8):
                times = scaled[0][later : later + 1, :]
                columns[later] = [c - s * times for c, s in zip(columns[later], scaled)]
            row = groups[b][j : j + 1, :]
            for before in range(j):
                row = row - columns[before][0][j : j + 1, :] * done[before]
            done.append(row * scale)
        for g in range(b + 1, 8):
            value = groups[g]
            for j in range(8):
                value = value - columns[j][g - b] * done[j]
            groups[g] = value
        for j in range(8):
            work[b * 8 + j : b * 8 + j + 1, :] = done[j]
    final = work[...]
    rows = lax.broadcasted_iota(jnp.int32, (K, 128), 0)
    lanes = lax.broadcasted_iota(jnp.int32, (K, 128), 1)
    upper = jnp.where(lanes - K >= rows, final, 0.0)
    factor[...] = upper.T[K:, :]
    inverse = final[:, :K]
    basis[...] = lax.dot_general(
        inverse,
        image[...],
        (((1,), (0,)), ((), ())),
        precision=lax.Precision.HIGHEST,
        preferred_element_type=F32,
    )


def orthogonalize(grams, image):
    vmem = pl.BlockSpec(memory_space=pltpu.VMEM)
    return pl.pallas_call(
        basis_kernel,
        in_specs=[vmem] * 5,
        out_specs=[vmem, vmem],
        out_shape=[
            jax.ShapeDtypeStruct((K, PIECE), F32),
            jax.ShapeDtypeStruct((K, K), F32),
        ],
        scratch_shapes=[pltpu.VMEM((K, 128), F32)],
        compiler_params=pltpu.CompilerParams(vmem_limit_bytes=16 * 1024 * 1024),
    )(*grams, image)


def shifted(value, axis, shift, size=4):
    return lax.ppermute(value, axis, [(i, (i + shift) % size) for i in range(size)])


def ring(a, b):
    return min((a - b) % 4, (b - a) % 4)


def placement():
    pairs, table = [], [0] * (8 * COLS)
    for y in range(4):
        for x in range(4):
            row = y * 2 + x // 2
            pieces = []
            for piece in range(8):
                from_y, from_x = 2 * (x % 2) + piece // 4, piece % 4
                pieces.append((-ring(from_y, y) - ring(from_x, x), piece, from_y * 4 + from_x))
            places = sorted((ring(z, y), z, core) for z in range(4) for core in range(2))
            for (_, piece, source), (_, z, core) in zip(sorted(pieces), places):
                target = (z * 2 + core) * COLS + y * 4 + x
                pairs.append((row * COLS + source, target))
                table[target] = piece
    return pairs, table


def gather_band(panel, rows):
    piece = transpose_panel(lax.ppermute(panel, AXES, placement()[0]), rows)
    own = jnp.stack([piece] + [shifted(piece, "z", turn) for turn in range(1, 4)])
    return own, shifted(own, "core", 1, 2)


def across(value, shift, first):
    pairs = []
    for z in range(4):
        for core in range(2):
            for y in range(4):
                for x in range(4):
                    along_x = (core == 0) == first
                    to = y * 4 + (x + shift) % 4 if along_x else (y + shift) % 4 * 4 + x
                    row = (z * 2 + core) * COLS
                    pairs.append((row + y * 4 + x, row + to))
    return lax.ppermute(value, AXES, pairs)


def sum_along(value, axis):
    near, across, far = (shifted(value, axis, shift) for shift in range(1, 4))
    return (value + across) + (near + far)


def per_device(panel, block_values, row_starts, block_columns, block_counts):
    values, rows, order = relayout_values(row_starts, block_counts, block_values)
    own, other = gather_band(panel, rows)
    partial = multiply(rows, block_columns, order, own, other, values)
    sums = stage_sums([partial[0]] + [across(partial[shift], shift, True) for shift in ORDER[:3]])
    arrived = [sums[0]] + [across(sums[shift], shift, False) for shift in (1, 2, 3)]
    image, gram = finish_image(arrived, panel)
    gram = jnp.sum(lax.all_to_all(gram, ("y", "x"), 0, 0, tiled=True), axis=0)
    gram = gram + shifted(gram, "core", 1, 2)
    grams = [gram] + [shifted(gram, "z", shift) for shift in range(1, 4)]
    basis, factor = orthogonalize(grams, image)
    return (basis, factor)


def solution(mesh):
    fine = Mesh(mesh.devices.reshape(4, 2, 4, 4), AXES)
    in_specs = (P(None, AXES), P(AXES, None), P(AXES), P(AXES), P(AXES))
    out_specs = (P(None, AXES), P())
    return jax.shard_map(
        per_device, mesh=fine, in_specs=in_specs, out_specs=out_specs, check_vma=False
    )
```

```python
import jax
import jax.numpy as jnp
from jax import lax
from jax.experimental import pallas as pl
from jax.experimental.pallas import tpu as pltpu
from jax.sharding import Mesh
from jax.sharding import PartitionSpec as P

K = 64
BS = 64
CAP = 512
RBLK = 256
CBLK = 128
PIECE = 1024
POINTS = 131072
COLS = 16
HALF = BS // 2
PART = 512
PITCH = 40
ORDER = (2, 1, 3, 0)
FIRST = 12
UNROLL = 128
AXES = ("z", "core", "y", "x")
F32 = jnp.float32
BF16 = jnp.bfloat16


def values_kernel(starts, counts, values, out, rows, order, spread):
    @pl.when(pl.program_id(0) == 0)
    def _():
        core, y, x = lax.axis_index("core"), lax.axis_index("y"), lax.axis_index("x")
        sub = lax.broadcasted_iota(jnp.int32, (8, 128), 0)
        lane = lax.broadcasted_iota(jnp.int32, (8, 128), 1)
        slots = sub * 128 + lane
        place = slots
        shift_rows = jnp.zeros_like(slots)
        live = slots < 0
        filled = 0
        steps = []
        for number in range(COLS):
            if number == FIRST:
                steps.append(lax.div(filled + UNROLL - 1, UNROLL))
                filled = steps[0] * UNROLL
            far, index = ORDER[number // 4], number % 4
            to_x, to_y = lax.rem(x + far, 4), lax.rem(y + far, 4)
            chunk = jnp.where(core == 0, index * 4 + to_x, to_y * 4 + index)
            low = starts[chunk * 16]
            after = starts[jnp.minimum(chunk * 16 + 16, RBLK - 1)]
            high = jnp.where(chunk == COLS - 1, counts[0], after)
            here = slots >= filled
            place = jnp.where(here, slots - filled + low, place)
            shift_rows = jnp.where(here, 16 * (number % FIRST) - 16 * chunk, shift_rows)
            live = jnp.logical_or(
                jnp.logical_and(live, jnp.logical_not(here)),
                jnp.logical_and(here, slots < filled + high - low),
            )
            filled = filled + high - low
        steps.append(lax.div(filled - steps[0] * UNROLL + UNROLL - 1, UNROLL))

        def count_up(step, total):
            for offset in range(8):
                total = total + jnp.where(place >= starts[step * 8 + offset], 1, 0)
            return total

        total = lax.fori_loop(0, RBLK // 8, count_up, jnp.full((8, 128), -1, jnp.int32))
        rows[...] = jnp.where(live, total + shift_rows, FIRST * 16)
        place = jnp.where(live, place, 0)
        order[...] = jnp.where(sub == 7, jnp.where(lane == 0, steps[0], steps[1]), place)

    for group in range(values.shape[0] // 16):
        for tile in range(HALF):
            part = values[group * 16 : (group + 1) * 16, tile * 128 : (tile + 1) * 128]
            spread[pl.ds(tile, 16, stride=PITCH), :] = part.astype(F32)
        for slot in range(16):
            first = (group * 16 + slot) * HALF
            block = spread[slot * PITCH : slot * PITCH + HALF, :]
            out[first : first + HALF, :] = block.astype(BF16)


def relayout_values(starts, counts, block_values):
    step = 64
    smem = pl.BlockSpec(memory_space=pltpu.SMEM)
    return pl.pallas_call(
        values_kernel,
        grid=(CAP // step,),
        in_specs=[smem, smem, pl.BlockSpec((step, BS * BS), lambda i: (i, 0))],
        out_specs=[
            pl.BlockSpec((step * HALF, 128), lambda i: (i, 0)),
            pl.BlockSpec((8, 128), lambda i: (0, 0)),
            pl.BlockSpec((8, 128), lambda i: (0, 0)),
        ],
        out_shape=[
            jax.ShapeDtypeStruct((CAP * HALF, 128), BF16),
            jax.ShapeDtypeStruct((8, 128), jnp.int32),
            jax.ShapeDtypeStruct((8, 128), jnp.int32),
        ],
        scratch_shapes=[pltpu.VMEM((16 * PITCH, 128), F32)],
        compiler_params=pltpu.CompilerParams(vmem_limit_bytes=16 * 1024 * 1024),
        cost_estimate=pl.CostEstimate(flops=0, bytes_accessed=24 * 1024 * 1024, transcendentals=0),
    )(starts, counts, block_values)


def transpose_kernel(panel, rows, out, work):
    work[:K, :] = panel[...].astype(F32)
    work[K:, :] = jnp.zeros_like(work[K:, :])
    points = work[...].T
    low = lax.broadcasted_iota(jnp.int32, (HALF, 128), 1) < BS
    for block in range(PIECE // BS):
        first = points[block * BS : block * BS + HALF, :]
        second = points[block * BS + HALF : (block + 1) * BS, :]
        pair = jnp.where(low, first, pltpu.roll(second, BS, 1))
        out[block * HALF : (block + 1) * HALF, :] = pair.astype(BF16)


def transpose_panel(panel, rows):
    vmem = pl.BlockSpec(memory_space=pltpu.VMEM)
    unread = pl.BlockSpec(memory_space=pl.ANY)
    return pl.pallas_call(
        transpose_kernel,
        in_specs=[vmem, unread],
        out_specs=vmem,
        out_shape=jax.ShapeDtypeStruct((PIECE // 2, 128), BF16),
        scratch_shapes=[pltpu.VMEM((128, PIECE), F32)],
        compiler_params=pltpu.CompilerParams(vmem_limit_bytes=16 * 1024 * 1024),
    )(panel, rows)


PIECE_ROWS = PIECE // BS * 128


def piece_place(turn, mine, table):
    z, core = lax.axis_index("z"), lax.axis_index("core")
    y, x = lax.axis_index("y"), lax.axis_index("x")
    side = core if mine else 1 - core
    return table[(lax.rem(z + 4 - turn, 4) * 2 + side) * COLS + y * 4 + x]


def fill_weights(band, place, weights):
    low = lax.broadcasted_iota(jnp.int32, (HALF, 128), 1) < BS
    zero = jnp.zeros((HALF, 128), F32)

    def fill(turn, carry):
        piece = place(turn)
        for block in range(PIECE // BS):
            pair = band[turn, block * HALF : (block + 1) * HALF, :].astype(F32)
            swapped = pltpu.roll(pair, BS, 1)
            tile = piece * (PIECE // BS) + block
            first = pl.multiple_of(tile * 128, 128)
            weights[pl.ds(first, HALF), :] = jnp.where(low, pair, zero).astype(BF16)
            weights[pl.ds(first + 32, HALF), :] = jnp.where(low, swapped, zero).astype(BF16)
            weights[pl.ds(first + 64, HALF), :] = jnp.where(low, zero, swapped).astype(BF16)
            weights[pl.ds(first + 96, HALF), :] = jnp.where(low, zero, pair).astype(BF16)
        return carry

    lax.fori_loop(0, 4, fill, 0)


def own_kernel(own, weights):
    fill_weights(own, lambda turn: turn, weights)


def own_weights(own):
    vmem = pl.BlockSpec(memory_space=pltpu.VMEM)
    return pl.pallas_call(
        own_kernel,
        in_specs=[vmem],
        out_specs=vmem,
        out_shape=jax.ShapeDtypeStruct((4 * PIECE_ROWS, 128), BF16),
        compiler_params=pltpu.CompilerParams(vmem_limit_bytes=16 * 1024 * 1024),
    )(own)


def add_products(first, steps, rows, order, tiles, values, weights, total):
    total[...] = jnp.zeros_like(total)

    def add_group(index, carry):
        group = (first + index) * UNROLL
        major, minor = lax.div(group, 128), lax.rem(group, 128)
        products = []
        for offset in range(UNROLL):
            slot = order[major, minor + offset]
            block = values[pl.ds(pl.multiple_of(slot * HALF, HALF), HALF), :]
            tile = weights[pl.ds(pl.multiple_of(tiles[slot] * 128, 128), 128), :]
            products.append(jnp.dot(block, tile, preferred_element_type=F32))
        for offset in range(UNROLL):
            where = pl.ds(pl.multiple_of(rows[major, minor + offset] * HALF, HALF), HALF)
            total[where, :] = total[where, :] + products[offset]
        return carry

    lax.fori_loop(0, steps, add_group, 0)


def write_chunks(total, outs):
    for number, out in enumerate(outs):
        for index in range(4):
            first = (number * 4 + index) * PART
            out[index] = total[first : first + PART, :].astype(BF16)


def first_kernel(rows, order, tiles, table, other, values, half, weights, out0, out1, out2, total, sems):
    copies = []
    for turn in range(4):
        first = pl.multiple_of(piece_place(turn, True, table) * PIECE_ROWS, PIECE_ROWS)
        source = half.at[pl.ds(turn * PIECE_ROWS, PIECE_ROWS), :]
        target = weights.at[pl.ds(first, PIECE_ROWS), :]
        copies.append(pltpu.make_async_copy(source, target, sems.at[turn]))
    for copy in copies:
        copy.start()
    fill_weights(other, lambda turn: piece_place(turn, False, table), weights)
    for copy in copies:
        copy.wait()
    add_products(0, order[7, 0], rows, order, tiles, values, weights, total)
    write_chunks(total, (out0, out1, out2))


def second_kernel(rows, order, tiles, weights, values, out0, total):
    add_products(order[7, 0], order[7, 1], rows, order, tiles, values, weights, total)
    write_chunks(total, (out0,))


def multiply(rows, tiles, order, own, other, values):
    smem = pl.BlockSpec(memory_space=pltpu.SMEM)
    vmem = pl.BlockSpec(memory_space=pltpu.VMEM)
    chunks = [jax.ShapeDtypeStruct((4, PART, 128), BF16)] * 3
    total = pltpu.VMEM(((FIRST * 16 + 1) * HALF, 128), F32)
    params = pltpu.CompilerParams(vmem_limit_bytes=16 * 1024 * 1024)
    table = jnp.array(placement()[1], jnp.int32)
    half = own_weights(own)
    weights, part2, part1, part3 = pl.pallas_call(
        first_kernel,
        in_specs=[smem] * 4 + [vmem] * 3,
        out_specs=[vmem] * 4,
        out_shape=[jax.ShapeDtypeStruct((CBLK * 128, 128), BF16)] + chunks,
        scratch_shapes=[total, pltpu.SemaphoreType.DMA((4,))],
        compiler_params=params,
    )(rows, order, tiles, table, other, values, half)
    (part0,) = pl.pallas_call(
        second_kernel,
        in_specs=[smem] * 3 + [vmem] * 2,
        out_specs=[vmem],
        out_shape=chunks[:1],
        scratch_shapes=[total],
        compiler_params=params,
        cost_estimate=pl.CostEstimate(flops=0, bytes_accessed=16 * 1024 * 1024, transcendentals=0),
    )(rows, order, tiles, weights, values)
    return part0, part1, part2, part3


def stage_kernel(*refs):
    ins, outs = refs[:4], refs[4:]
    base = jnp.where(lax.axis_index("core") == 0, lax.axis_index("y"), lax.axis_index("x"))
    for shift in range(4):
        to = lax.rem(base + shift, 4)
        total = ins[0][to].astype(F32)
        for index in range(1, 4):
            total = total + ins[index][to].astype(F32)
        outs[shift][...] = total.astype(outs[shift].dtype)


def stage_sums(arrays):
    vmem = pl.BlockSpec(memory_space=pltpu.VMEM)
    shapes = [jax.ShapeDtypeStruct((PART, 128), F32)]
    shapes += [jax.ShapeDtypeStruct((PART, 128), BF16)] * 3
    return pl.pallas_call(
        stage_kernel,
        in_specs=[vmem] * 4,
        out_specs=[vmem] * 4,
        out_shape=shapes,
        compiler_params=pltpu.CompilerParams(vmem_limit_bytes=16 * 1024 * 1024),
    )(*arrays)


def image_kernel(*refs):
    ins, (panel, image, gram, spread, packed) = refs[:4], refs[4:]
    total = ins[0][...]
    for index in range(1, 4):
        total = total + ins[index][...].astype(F32)
    spread[pl.ds(0, PART, stride=2), :] = total
    spread[pl.ds(1, PART, stride=2), :] = pltpu.roll(total, BS, 1)
    whole = spread[...].T[:K, :] + panel[...].astype(F32)
    image[...] = whole
    product = lax.dot_general(
        whole,
        whole,
        (((1,), (1,)), ((), ())),
        precision=lax.Precision.HIGHEST,
        preferred_element_type=F32,
    ) * (1.0 / POINTS)
    packed[:, :K] = product[: K // 2, :]
    packed[:, K:] = product[K // 2 :, :]
    for index in range(COLS):
        gram[index] = packed[...]


def finish_image(arrays, panel):
    vmem = pl.BlockSpec(memory_space=pltpu.VMEM)
    return pl.pallas_call(
        image_kernel,
        in_specs=[vmem] * 5,
        out_specs=[vmem, vmem],
        out_shape=[
            jax.ShapeDtypeStruct((K, PIECE), F32),
            jax.ShapeDtypeStruct((COLS, K // 2, 128), F32),
        ],
        scratch_shapes=[pltpu.VMEM((PIECE, 128), F32), pltpu.VMEM((K // 2, 128), F32)],
        compiler_params=pltpu.CompilerParams(vmem_limit_bytes=16 * 1024 * 1024),
    )(*arrays, panel)


def basis_kernel(g0, g1, g2, g3, image, basis, factor, work):
    gram = (g0[...] + g2[...]) + (g1[...] + g3[...])
    work[...] = jnp.zeros_like(work)
    work[: K // 2, :K] = gram[:, :K]
    work[K // 2 :, :K] = pltpu.roll(gram, K, 1)[:, :K]
    lane = lax.broadcasted_iota(jnp.int32, (8, 128), 1)
    sub = lax.broadcasted_iota(jnp.int32, (8, 128), 0)
    groups = []
    for g in range(8):
        shifted = pltpu.roll(work[g * 8 : (g + 1) * 8, :], K, 1)
        groups.append(jnp.where(lane == sub + g * 8, 1.0, shifted))
    for b in range(8):
        columns = []
        for j in range(8):
            at = K + b * 8 + j
            columns.append(
                [jnp.broadcast_to(groups[g][:, at : at + 1], (8, 128)) for g in range(b, 8)]
            )
        done = []
        for j in range(8):
            scale = lax.rsqrt(columns[j][0][j : j + 1, :])
            scaled = [c * scale for c in columns[j]]
            columns[j] = scaled
            for later in range(j + 1, 8):
                times = scaled[0][later : later + 1, :]
                columns[later] = [c - s * times for c, s in zip(columns[later], scaled)]
            row = groups[b][j : j + 1, :]
            for before in range(j):
                row = row - columns[before][0][j : j + 1, :] * done[before]
            done.append(row * scale)
        for g in range(b + 1, 8):
            value = groups[g]
            for j in range(8):
                value = value - columns[j][g - b] * done[j]
            groups[g] = value
        for j in range(8):
            work[b * 8 + j : b * 8 + j + 1, :] = done[j]
    final = work[...]
    rows = lax.broadcasted_iota(jnp.int32, (K, 128), 0)
    lanes = lax.broadcasted_iota(jnp.int32, (K, 128), 1)
    upper = jnp.where(lanes - K >= rows, final, 0.0)
    factor[...] = upper.T[K:, :]
    inverse = final[:, :K]
    basis[...] = lax.dot_general(
        inverse,
        image[...],
        (((1,), (0,)), ((), ())),
        precision=lax.Precision.HIGHEST,
        preferred_element_type=F32,
    )


def orthogonalize(grams, image):
    vmem = pl.BlockSpec(memory_space=pltpu.VMEM)
    return pl.pallas_call(
        basis_kernel,
        in_specs=[vmem] * 5,
        out_specs=[vmem, vmem],
        out_shape=[
            jax.ShapeDtypeStruct((K, PIECE), F32),
            jax.ShapeDtypeStruct((K, K), F32),
        ],
        scratch_shapes=[pltpu.VMEM((K, 128), F32)],
        compiler_params=pltpu.CompilerParams(vmem_limit_bytes=16 * 1024 * 1024),
    )(*grams, image)


def shifted(value, axis, shift, size=4):
    return lax.ppermute(value, axis, [(i, (i + shift) % size) for i in range(size)])


def ring(a, b):
    return min((a - b) % 4, (b - a) % 4)


def placement():
    pairs, table = [], [0] * (8 * COLS)
    for y in range(4):
        for x in range(4):
            row = y * 2 + x // 2
            pieces = []
            for piece in range(8):
                from_y, from_x = 2 * (x % 2) + piece // 4, piece % 4
                pieces.append((-ring(from_y, y) - ring(from_x, x), piece, from_y * 4 + from_x))
            places = sorted((ring(z, y), z, core) for z in range(4) for core in range(2))
            for (_, piece, source), (_, z, core) in zip(sorted(pieces), places):
                target = (z * 2 + core) * COLS + y * 4 + x
                pairs.append((row * COLS + source, target))
                table[target] = piece
    return pairs, table


def gather_band(panel, rows):
    piece = transpose_panel(lax.ppermute(panel, AXES, placement()[0]), rows)
    own = jnp.stack([piece] + [shifted(piece, "z", turn) for turn in range(1, 4)])
    return own, shifted(own, "core", 1, 2)


def across(value, shift, first):
    pairs = []
    for z in range(4):
        for core in range(2):
            for y in range(4):
                for x in range(4):
                    along_x = (core == 0) == first
                    to = y * 4 + (x + shift) % 4 if along_x else (y + shift) % 4 * 4 + x
                    row = (z * 2 + core) * COLS
                    pairs.append((row + y * 4 + x, row + to))
    return lax.ppermute(value, AXES, pairs)


def sum_along(value, axis):
    near, across, far = (shifted(value, axis, shift) for shift in range(1, 4))
    return (value + across) + (near + far)


def per_device(panel, block_values, row_starts, block_columns, block_counts):
    values, rows, order = relayout_values(row_starts, block_counts, block_values)
    own, other = gather_band(panel, rows)
    partial = multiply(rows, block_columns, order, own, other, values)
    sums = stage_sums([partial[0]] + [across(partial[shift], shift, True) for shift in ORDER[:3]])
    arrived = [sums[0]] + [across(sums[shift], shift, False) for shift in ORDER[:3]]
    image, gram = finish_image(arrived, panel)
    gram = jnp.sum(lax.all_to_all(gram, ("y", "x"), 0, 0, tiled=True), axis=0)
    gram = gram + shifted(gram, "core", 1, 2)
    grams = [gram] + [shifted(gram, "z", shift) for shift in range(1, 4)]
    basis, factor = orthogonalize(grams, image)
    return (basis, factor)


def solution(mesh):
    fine = Mesh(mesh.devices.reshape(4, 2, 4, 4), AXES)
    in_specs = (P(None, AXES), P(AXES, None), P(AXES), P(AXES), P(AXES))
    out_specs = (P(None, AXES), P())
    return jax.shard_map(
        per_device, mesh=fine, in_specs=in_specs, out_specs=out_specs, check_vma=False
    )
```
